128 devices in a mesh: ens: 8 (over x, y_hi), space: 16 (over y_lo, z, core).
Axes of the slice: x: 4, y: 4 (y_hi: 2, y_lo: 2; y = y_hi * 2 + y_lo), z: 4, core: 2. Of those that a mesh axis runs over, the one named last changes fastest.
Arguments:
- states: bfloat16 [16, 8192, 1024], P('ens', 'space'), may hold values from -6 to 6
- member_noise: float32 [16, 1024], P('ens')
- w_query: bfloat16 [1024, 1024], replicated, may hold values from -1 to 1
- w_key: bfloat16 [1024, 1024], replicated, may hold values from -1 to 1
- w_value: bfloat16 [1024, 1024], replicated, may hold values from -0.1875 to 0.1875
- w_out: bfloat16 [1024, 1024], replicated, may hold values from -0.1875 to 0.1875
- w_decode: bfloat16 [1024, 128], replicated, may hold values from -0.1875 to 0.1875
- target: float32 [8192, 128], P('space')
Outputs:
- state_grad: bfloat16 [16, 8192, 1024], P('ens', 'space')
- loss: float32 [], replicated
The draws below stay inside these ranges and needn't reach their ends.
All inputs are finite; a program needn't handle non-finite values.
Results may differ from the reference program's by a relative error of at most 0.014.
Values may be sent and summed in bfloat16 or wider, within the bound.
No kernel may reach another device: no remote copies, remote signals or barrier semaphores. Data moves between devices by JAX's collectives and lax.ppermute only.
A program may use at most 192 MiB of HBM per device.

```python
import math
import jax
import jax.numpy as jnp
from jax import lax

D = 1024
HEADS = 16
VARS = 128
WIN = 256
MEMBERS = 16
NODES = 8192


def drawn_weight(key):
    base_part = jax.random.normal(key, (D, D), jnp.float32) / math.sqrt(D)
    return jnp.clip(base_part, -6.0 / math.sqrt(D), 6.0 / math.sqrt(D))


def draw_w_query(key, part):
    key = jax.random.fold_in(key, 31)
    return drawn_weight(key).astype(jnp.bfloat16)


def draw_w_key(key, part):
    key = jax.random.fold_in(key, 37)
    return drawn_weight(key).astype(jnp.bfloat16)


def draw_states(key, part):
    key = jax.random.fold_in(key, 41)
    bulk_key = jax.random.fold_in(key, 0)
    return jnp.clip(jax.random.normal(bulk_key, (MEMBERS, NODES, D), jnp.float32), -6.0, 6.0).astype(jnp.bfloat16)


def draw_member_noise(key, part):
    key = jax.random.fold_in(key, 11)
    rising = 0.5 + jnp.arange(MEMBERS, dtype=jnp.float32)[:, None] / (MEMBERS - 1)
    base = jax.random.normal(key, (MEMBERS, D), jnp.float32)
    return base * rising


def draw_target(key, part):
    key = jax.random.fold_in(key, 23)
    place = jnp.arange(NODES, dtype=jnp.float32)[:, None] / NODES
    rising = 0.6 * jnp.exp(place * math.log(3.0))
    first_key = jax.random.fold_in(key, 0)
    base = jax.random.normal(first_key, (NODES, VARS), jnp.float32)
    return base * rising


def normal_values(own_key, dims, deviation, reach, kind=jnp.bfloat16):
    values = deviation * jax.random.normal(own_key, dims, jnp.float32)
    return jnp.clip(values, min=-reach, max=reach).astype(kind)


def setup_inputs(seed: int = 0) -> dict:
    seeds = jax.random.split(jax.random.key(seed), 9)
    states = draw_states(jax.random.fold_in(seeds[8], 71), 0)
    member_noise = draw_member_noise(jax.random.fold_in(seeds[8], 71), 0)
    w_query = draw_w_query(jax.random.fold_in(seeds[8], 71), 0)
    w_key = draw_w_key(jax.random.fold_in(seeds[8], 71), 0)
    w_value = normal_values(seeds[4], (D, D), D ** -0.5, 0.1875)
    w_out = normal_values(seeds[5], (D, D), D ** -0.5, 0.1875)
    w_decode = normal_values(seeds[6], (D, VARS), D ** -0.5, 0.1875)
    target = draw_target(jax.random.fold_in(seeds[8], 71), 0)
    return {"states": states, "member_noise": member_noise, "w_query": w_query, "w_key": w_key, "w_value": w_value, "w_out": w_out, "w_decode": w_decode, "target": target}


SMOOTH = 0.25

def slope(delta):
    return delta * lax.rsqrt(delta * delta + SMOOTH * SMOOTH)

def spread_of(delta):
    return jnp.sqrt(delta * delta + SMOOTH * SMOOTH)

def project(source, weight):
    return jnp.dot(source, weight, preferred_element_type=jnp.float32).astype(jnp.bfloat16)

def attend(query_block, keys, values, start, total):
    row_count, width = query_block.shape
    block = min(512, row_count)
    count = row_count // block
    depth = width // HEADS

    def one_block(index):
        first = (index * block).astype(jnp.int32)
        query_piece = lax.dynamic_slice_in_dim(query_block, first, block, 0).reshape(block, HEADS, depth).astype(jnp.float32)
        key_piece = lax.dynamic_slice_in_dim(keys, first, block + 2 * WIN, 0).reshape(block + 2 * WIN, HEADS, depth).astype(jnp.float32)
        value_piece = lax.dynamic_slice_in_dim(values, first, block + 2 * WIN, 0).reshape(block + 2 * WIN, HEADS, depth).astype(jnp.float32)
        scores = jnp.einsum('qhd,khd->hqk', query_piece, key_piece) / math.sqrt(depth)
        query_pos = start + first + jnp.arange(block, dtype=jnp.int32)
        key_pos = start + first - WIN + jnp.arange(block + 2 * WIN, dtype=jnp.int32)
        near = (jnp.abs(query_pos[:, None] - key_pos[None, :]) <= WIN) & (key_pos[None, :] >= 0) & (key_pos[None, :] < total)
        scores = jnp.where(near[None], scores, -1e+30)
        top = lax.optimization_barrier(jnp.max(scores, axis=-1, keepdims=True))
        expo = jnp.exp(scores - top)
        weights = (expo / lax.optimization_barrier(jnp.sum(expo, axis=-1, keepdims=True))).astype(jnp.bfloat16)
        mixed = jnp.einsum('hqk,khd->qhd', weights.astype(jnp.float32), value_piece)
        return mixed.astype(jnp.bfloat16).reshape(block, width)
    return lax.map(one_block, jnp.arange(count, dtype=jnp.int32)).reshape(row_count, width)

def reference(states, member_noise, w_query, w_key, w_value, w_out, w_decode, target):
    hidden_state = states.astype(jnp.float32) + member_noise[:, None, :]
    normalized_state = (hidden_state * lax.rsqrt(lax.optimization_barrier(jnp.mean(hidden_state * hidden_state, axis=-1, keepdims=True)) + 1e-05)).astype(jnp.bfloat16)
    padding = jnp.zeros((WIN, D), jnp.bfloat16)

    def member_state(items):
        hid, nrm = items
        query_block = project(nrm, w_query)
        keys = jnp.concatenate([padding, project(nrm, w_key), padding], axis=0)
        values = jnp.concatenate([padding, project(nrm, w_value), padding], axis=0)
        mixed = attend(query_block, keys, values, 0, NODES)
        updated = (hid + jnp.dot(mixed, w_out, preferred_element_type=jnp.float32)).astype(jnp.bfloat16)
        return jnp.dot(updated, w_decode, preferred_element_type=jnp.float32).astype(jnp.bfloat16)
    predict_states = lax.map(member_state, (hidden_state, normalized_state))
    member_group = predict_states.astype(jnp.float32)

    def fair_score(one):
        self_term = one.astype(jnp.float32)
        miss = self_term - target
        differ = self_term[None] - member_group
        loss_gradient = slope(miss) - lax.optimization_barrier(jnp.sum(slope(differ), axis=0)) / (MEMBERS - 1)
        local = jnp.sum(spread_of(miss)) - jnp.sum(spread_of(differ)) / (2 * (MEMBERS - 1))
        return (loss_gradient.astype(jnp.bfloat16), local)
    prediction_gradient, gathered_locals = lax.map(fair_score, predict_states)
    loss = jnp.sum(gathered_locals) / (MEMBERS * NODES * VARS)

    def backward(grad_one):
        return jnp.dot(grad_one, w_decode.T, preferred_element_type=jnp.float32).astype(jnp.bfloat16)
    state_grad = lax.map(backward, prediction_gradient)
    return (state_grad, loss)
```

```python
import functools
import math

import jax
import jax.numpy as jnp
from jax import lax
from jax.experimental import pallas as pl
from jax.experimental.pallas import tpu as pltpu
from jax.sharding import PartitionSpec as P

HEADS = 16
WIN = 256
SMOOTH = 0.25
EPS = 1e-5
SUB = 128
UNROLL = 4
LOW, HIGH = 2.0**-80, 2.0**100
BF, F32 = jnp.bfloat16, jnp.float32
VMEM = pl.BlockSpec(memory_space=pltpu.VMEM)
NT = (((1,), (1,)), ((), ()))


def params():
    return pltpu.CompilerParams(vmem_limit_bytes=56 * 2**20)


def normed(rows, noise):
    hidden = rows.astype(F32) + noise
    return (hidden * lax.rsqrt(jnp.mean(hidden * hidden, axis=-1, keepdims=True) + EPS)).astype(BF)


def qkv_kernel(states, noise, w_query, w_key, w_value, query, keys, values, norm):
    members, rows, width = states.shape
    scale = math.log2(math.e) / math.sqrt(width // HEADS)

    @pl.when(pl.program_id(0) == 0)
    def _():
        for m in range(members):

            def piece(i, _):
                at = pl.ds(pl.multiple_of(i * SUB, SUB), SUB)
                norm[m, at] = normed(states[m, at], noise[m])
                return 0

            lax.fori_loop(0, rows // SUB, piece, 0)

    for m in range(members):
        x = norm[m]
        query[m] = (jnp.dot(x, w_query[...], preferred_element_type=F32) * scale).astype(BF)
        keys[m] = jnp.dot(x, w_key[...], preferred_element_type=F32).astype(BF)
        values[m] = jnp.dot(x, w_value[...], preferred_element_type=F32).astype(BF)


def qkv(states, noise, w_query, w_key, w_value):
    members, rows, width = states.shape
    cols = 256
    weight = pl.BlockSpec((width, cols), lambda j: (0, j))
    out = pl.BlockSpec((members, rows, cols), lambda j: (0, 0, j))
    return pl.pallas_call(
        qkv_kernel,
        grid=(width // cols,),
        out_shape=[jax.ShapeDtypeStruct(states.shape, BF)] * 3,
        in_specs=[
            pl.BlockSpec(states.shape, lambda j: (0, 0, 0)),
            pl.BlockSpec(noise.shape, lambda j: (0, 0, 0)),
            weight,
            weight,
            weight,
        ],
        out_specs=[out] * 3,
        scratch_shapes=[pltpu.VMEM(states.shape, BF)],
        compiler_params=params(),
        cost_estimate=pl.CostEstimate(
            flops=6 * members * rows * width * width, bytes_accessed=8 * 2**20, transcendentals=0
        ),
        name="own_qkv",
    )(states, noise, w_query, w_key, w_value)


def attend_kernel(
    place, states, noise, above, below, query, keys, values, w_key, w_value, w_out, w_decode,
    forecast, norm, halo_k, halo_v, kk, vv, mixed, bad,
):
    members, rows, width = states.shape
    pairs = width // SUB
    subs = rows // SUB
    pad = WIN // SUB
    span = 2 * pad + 1
    total = subs + 2 * pad
    lane = lax.broadcasted_iota(jnp.int32, (SUB, SUB), 1)
    row = lax.broadcasted_iota(jnp.int32, (SUB, SUB), 0)
    left = lane < SUB // 2
    zero = jnp.zeros((SUB, SUB), BF)
    one = jnp.ones((SUB, SUB), BF)
    starts = place[0] == 0
    ends = place[0] == place[1] - 1

    def absent(j):
        return starts if j < pad else ends

    def outside(j):
        return j < pad or j >= pad + subs

    for u in range(UNROLL):
        for j in range(total):
            unit = jnp.where(absent(j), zero, one) if outside(j) else one
            at = 2 * SUB * j
            vv[u, at : at + SUB, SUB:] = jnp.where(left, unit, zero)
            vv[u, at + SUB : at + 2 * SUB, SUB:] = jnp.where(left, zero, unit)

    def source(m, inner, halo, j, c):
        if j < pad:
            return halo[j * SUB : (j + 1) * SUB, c]
        if j < pad + subs:
            return inner[m, (j - pad) * SUB : (j - pad + 1) * SUB, c]
        return halo[(j - subs) * SUB : (j - subs + 1) * SUB, c]

    def pack(m, u, pair):
        c = pl.ds(pl.multiple_of(pair * SUB, SUB), SUB)
        for j in range(total):
            at = 2 * SUB * j
            key = source(m, keys, halo_k, j, c)
            value = source(m, values, halo_v, j, c)
            if outside(j):
                value = jnp.where(absent(j), zero, value)
            kk[u, at : at + SUB] = jnp.where(left, key, zero)
            kk[u, at + SUB : at + 2 * SUB] = jnp.where(left, zero, key)
            vv[u, at : at + SUB, :SUB] = jnp.where(left, value, zero)
            vv[u, at + SUB : at + 2 * SUB, :SUB] = jnp.where(left, zero, value)

    def masked(s, j):
        if j == 0:
            return jnp.where(lane >= row, s, -1e30)
        if j == span - 1:
            return jnp.where(lane <= row, s, -1e30)
        return s

    def block(m, u, pair, a):
        c = pl.ds(pl.multiple_of(pair * SUB, SUB), SUB)
        at = slice(2 * SUB * a, 2 * SUB * (a + span))
        s = lax.dot_general(
            query[m, a * SUB : (a + 1) * SUB, c], kk[u, at], NT, preferred_element_type=F32
        )
        parts = []
        for j in range(2 * span):
            parts.append(jnp.exp2(masked(s[:, j * SUB : (j + 1) * SUB], j // 2)).astype(BF))
        o = jnp.dot(jnp.concatenate(parts, axis=1), vv[u, at], preferred_element_type=F32)
        norms = o[:, SUB:]
        mixed[a * SUB : (a + 1) * SUB, c] = (o[:, :SUB] / norms).astype(BF)
        bad[...] = jnp.where((norms > LOW) & (norms < HIGH), bad[...], 1.0)

    def safe_block(m, pair, a):
        c = pl.ds(pl.multiple_of(pair * SUB, SUB), SUB)
        q = query[m, a * SUB : (a + 1) * SUB, c]
        outs = []
        for side in range(2):
            mine = left if side == 0 else ~left
            scores, vals = [], []
            for j in range(a, a + span):
                key = source(m, keys, halo_k, j, c)
                s = lax.dot_general(
                    jnp.where(mine, q, zero), key, NT, preferred_element_type=F32
                )
                s = masked(s, j - a)
                if outside(j):
                    s = jnp.where(absent(j), -1e30, s)
                scores.append(s)
                vals.append(source(m, values, halo_v, j, c))
            s = jnp.concatenate(scores, axis=1)
            p = jnp.exp2(s - jnp.max(s, axis=-1, keepdims=True))
            norms = jnp.sum(p, axis=-1, keepdims=True)
            outs.append(
                jnp.dot(
                    (p / norms).astype(BF),
                    jnp.concatenate(vals, axis=0),
                    preferred_element_type=F32,
                )
            )
        mixed[a * SUB : (a + 1) * SUB, c] = jnp.where(left, outs[0], outs[1]).astype(BF)

    def member(m, _):
        for i in range(pad):
            at = slice(i * SUB, (i + 1) * SUB)
            norm[at] = normed(above[m, at], noise[m])
            norm[WIN + i * SUB : WIN + (i + 1) * SUB] = normed(below[m, at], noise[m])

        def halo(i, _):
            c = pl.ds(pl.multiple_of(i * 256, 256), 256)
            halo_k[:, c] = jnp.dot(norm[...], w_key[:, c], preferred_element_type=F32).astype(BF)
            halo_v[:, c] = jnp.dot(norm[...], w_value[:, c], preferred_element_type=F32).astype(BF)
            return 0

        lax.fori_loop(0, width // 256, halo, 0)
        bad[...] = jnp.zeros_like(bad)

        def heads(i, _):
            for u in range(UNROLL):
                pack(m, u, i * UNROLL + u)
            for u in range(UNROLL):
                for a in range(subs):
                    block(m, u, i * UNROLL + u, a)
            return 0

        lax.fori_loop(0, pairs // UNROLL, heads, 0)

        @pl.when(jnp.max(bad[...]) > 0.0)
        def _():
            def again(pair, _):
                for a in range(subs):
                    safe_block(m, pair, a)
                return 0

            lax.fori_loop(0, pairs, again, 0)

        for i in range(rows // 256):
            at = slice(i * 256, (i + 1) * 256)
            hidden = states[m, at].astype(F32) + noise[m]
            updated = hidden + jnp.dot(mixed[at], w_out[...], preferred_element_type=F32)
            out = jnp.dot(updated.astype(BF), w_decode[...], preferred_element_type=F32)
            share = rows // forecast.shape[0]
            each = 256 // share
            forecast[i * each : (i + 1) * each, m] = out.astype(BF).reshape(each, share, -1)
        return 0

    lax.fori_loop(0, members, member, 0)


def attend(place, states, noise, above, below, query, keys, values, w_key, w_value, w_out, w_decode, shares):
    members, rows, width = states.shape
    held = 2 * WIN + rows
    return pl.pallas_call(
        attend_kernel,
        out_shape=jax.ShapeDtypeStruct((shares, members, rows // shares, w_decode.shape[1]), BF),
        in_specs=[pl.BlockSpec(memory_space=pltpu.SMEM)] + [VMEM] * 11,
        out_specs=VMEM,
        scratch_shapes=[
            pltpu.VMEM((2 * WIN, width), BF),
            pltpu.VMEM((2 * WIN, width), BF),
            pltpu.VMEM((2 * WIN, width), BF),
            pltpu.VMEM((UNROLL, 2 * held, SUB), BF),
            pltpu.VMEM((UNROLL, 2 * held, 2 * SUB), BF),
            pltpu.VMEM((rows, width), BF),
            pltpu.VMEM((SUB, SUB), F32),
        ],
        compiler_params=params(),
        cost_estimate=pl.CostEstimate(
            flops=24 * members * rows * width * width // 2,
            bytes_accessed=20 * 2**20,
            transcendentals=members * rows * HEADS * 640,
        ),
        name="window_attention",
    )(place, states, noise, above, below, query, keys, values, w_key, w_value, w_out, w_decode)


def crps_kernel(place, gathered, target, grad, partial):
    groups, local, share, lanes = gathered.shape
    members = groups * local
    first = place[2] * share

    def piece(i, total):
        at = pl.ds(pl.multiple_of(i * 16, 16), 16)
        out = []
        for half in range(2):
            cut = slice(half * 8, half * 8 + 8)
            goal = target[pl.ds(pl.multiple_of(first + i * 16 + half * 8, 8), 8)]
            pred = [gathered[m // local, m % local, at].astype(F32)[cut] for m in range(members)]
            slopes = [None] * members
            spread = jnp.zeros_like(goal)
            pull = []
            for a in range(members):
                delta = pred[a] - goal
                square = delta * delta + SMOOTH * SMOOTH
                inv = lax.rsqrt(square)
                pull.append(delta * inv)
                total = total + square * inv
                for b in range(a + 1, members):
                    delta = pred[a] - pred[b]
                    square = delta * delta + SMOOTH * SMOOTH
                    inv = lax.rsqrt(square)
                    f = delta * inv
                    spread = spread + square * inv
                    slopes[a] = f if slopes[a] is None else slopes[a] + f
                    slopes[b] = -f if slopes[b] is None else slopes[b] - f
            total = total - (2.0 * spread + members * SMOOTH) / (2 * (members - 1))
            out.append([pull[a] - slopes[a] / (members - 1) for a in range(members)])
        for m in range(members):
            grad[m // local, m % local, at] = jnp.concatenate([out[0][m], out[1][m]], 0).astype(BF)
        return total

    total = lax.fori_loop(0, share // 16, piece, jnp.zeros((8, lanes), F32))
    partial[...] = jnp.sum(total, axis=0, keepdims=True)


def crps(place, gathered, target):
    return pl.pallas_call(
        crps_kernel,
        out_shape=[
            jax.ShapeDtypeStruct(gathered.shape, BF),
            jax.ShapeDtypeStruct((1, gathered.shape[-1]), F32),
        ],
        in_specs=[pl.BlockSpec(memory_space=pltpu.SMEM), VMEM, VMEM],
        out_specs=[VMEM, VMEM],
        compiler_params=params(),
        name="fair_crps",
    )(place, gathered, target)


def back_kernel(slopes, w_decode, grad):
    shares, _, share, lanes = slopes.shape
    rows = slopes[:, 0].reshape(shares * share, lanes)
    grad[0] = lax.dot_general(rows, w_decode[...], NT, preferred_element_type=F32).astype(BF)


def back(slopes, w_decode):
    shares, members, share, lanes = slopes.shape
    width = w_decode.shape[0]
    cols = 512
    return pl.pallas_call(
        back_kernel,
        grid=(members, width // cols),
        out_shape=jax.ShapeDtypeStruct((members, shares * share, width), BF),
        in_specs=[
            pl.BlockSpec((shares, 1, share, lanes), lambda m, j: (0, m, 0, 0)),
            pl.BlockSpec((cols, lanes), lambda m, j: (j, 0)),
        ],
        out_specs=pl.BlockSpec((1, shares * share, cols), lambda m, j: (m, 0, j)),
        compiler_params=params(),
        cost_estimate=pl.CostEstimate(
            flops=2 * members * shares * share * width * lanes,
            bytes_accessed=3 * 2**20,
            transcendentals=0,
        ),
        name="state_grad",
    )(slopes, w_decode)


def body(states, member_noise, w_query, w_key, w_value, w_out, w_decode, target):
    members, rows, width = states.shape
    ens, space = lax.axis_size("ens"), lax.axis_size("space")
    place = jnp.stack([lax.axis_index("space"), jnp.int32(space), lax.axis_index("ens")])
    noise = member_noise[:, None, :]
    up = [(i, i + 1) for i in range(space - 1)]
    down = [(i + 1, i) for i in range(space - 1)]
    above = lax.ppermute(states[:, rows - WIN :], "space", up)
    below = lax.ppermute(states[:, :WIN], "space", down)
    query, keys, values = qkv(states, noise, w_query, w_key, w_value)
    forecast = attend(
        place, states, noise, above, below, query, keys, values, w_key, w_value, w_out, w_decode, ens
    )
    gathered = lax.all_to_all(forecast, "ens", 0, 0)
    slopes, partial = crps(place, gathered, target)
    mine = lax.all_to_all(slopes, "ens", 0, 0)
    parts = lax.all_to_all(
        jnp.broadcast_to(partial, (ens * space, 1, partial.shape[-1])), ("ens", "space"), 0, 0
    )
    loss = jnp.sum(parts) / (members * ens * rows * space * w_decode.shape[1])
    return back(mine, w_decode), loss


def solution(mesh):
    in_specs = (P("ens", "space", None), P("ens", None), P(), P(), P(), P(), P(), P("space", None))
    out_specs = (P("ens", "space", None), P())
    return jax.shard_map(body, mesh=mesh, in_specs=in_specs, out_specs=out_specs, check_vma=False)
```

```python
import functools
import math

import jax
import jax.numpy as jnp
from jax import lax
from jax.experimental import pallas as pl
from jax.experimental.pallas import tpu as pltpu
from jax.sharding import PartitionSpec as P

HEADS = 16
WIN = 256
SMOOTH = 0.25
EPS = 1e-5
LOG2E = math.log2(math.e)
SUB = 128
UNROLL = 4
TAIL = 16
LOW, HIGH = 2.0**-80, 2.0**100
BF, F32 = jnp.bfloat16, jnp.float32
VMEM = pl.BlockSpec(memory_space=pltpu.VMEM)
HBM = pl.BlockSpec(memory_space=pltpu.HBM)
NT = (((1,), (1,)), ((), ()))


def params(mib):
    return pltpu.CompilerParams(vmem_limit_bytes=mib * 2**20)


def normed(rows, noise):
    hidden = rows.astype(F32) + noise
    return (hidden * lax.rsqrt(jnp.mean(hidden * hidden, axis=-1, keepdims=True) + EPS)).astype(BF)


def split(x, terms):
    parts = []
    for _ in range(terms):
        parts.append(x.astype(BF))
        x = x - parts[-1].astype(F32)
    return parts


def edges_kernel(states, far, near, sems):
    rows = states.shape[1]
    even = lax.axis_index("space") % 2 == 0
    first, last = pl.ds(0, WIN), pl.ds(rows - WIN, WIN)

    def move(out, back):
        copies = [
            pltpu.make_async_copy(states.at[0, out], far, sems.at[0]),
            pltpu.make_async_copy(states.at[:, back], near, sems.at[1]),
        ]
        for copy in copies:
            copy.start()
        for copy in copies:
            copy.wait()

    @pl.when(even)
    def _():
        move(first, last)

    @pl.when(~even)
    def _():
        move(last, first)


def edges(states):
    members, _, width = states.shape
    return pl.pallas_call(
        edges_kernel,
        out_shape=[
            jax.ShapeDtypeStruct((WIN, width), BF),
            jax.ShapeDtypeStruct((members, WIN, width), BF),
        ],
        in_specs=[HBM],
        out_specs=[VMEM] * 2,
        scratch_shapes=[pltpu.SemaphoreType.DMA((2,))],
        compiler_params=params(4),
        name="edges",
    )(pltpu.with_memory_space_constraint(states, pltpu.HBM))


def qkv_kernel(
    states, noise, w_query, w_key, w_value, query, keys, values, far, held_key, held_value,
    norm, shift, held_query, sems,
):
    members, rows, width = states.shape
    even = lax.axis_index("space") % 2 == 0
    scale = 1.0 / math.sqrt(width // HEADS)
    step = 256
    pieces = [(m, pl.ds(i * step, step)) for m in range(members) for i in range(rows // step)]
    moves = [(noise, shift), (w_query, held_query), (w_key, held_key), (w_value, held_value)]
    copies = [pltpu.make_async_copy(a, b, sems.at[i]) for i, (a, b) in enumerate(moves)]
    copies[0].start()
    copies[1].start()
    copies[0].wait()
    for m, at in pieces[:1]:
        norm[m, at] = normed(states[m, at], shift[m : m + 1])
    copies[1].wait()
    copies[2].start()
    copies[3].start()
    for i, (m, at) in enumerate(pieces):
        x = norm[m, at]
        query[m, at] = (jnp.dot(x, held_query[...], preferred_element_type=F32) * scale).astype(BF)
        for later, part in pieces[i + 1 : i + 2]:
            norm[later, part] = normed(states[later, part], shift[later : later + 1])
    for m in range(1, members):
        far[m - 1] = jnp.where(even, states[m, :WIN], states[m, rows - WIN :])
    copies[2].wait()
    for m, at in pieces:
        keys[m, at] = jnp.dot(norm[m, at], held_key[...], preferred_element_type=F32).astype(BF)
    copies[3].wait()
    for m, at in pieces:
        values[m, at] = jnp.dot(norm[m, at], held_value[...], preferred_element_type=F32).astype(BF)


def qkv(states, noise, w_query, w_key, w_value):
    members, rows, width = states.shape
    return pl.pallas_call(
        qkv_kernel,
        out_shape=[jax.ShapeDtypeStruct(states.shape, BF)] * 3
        + [jax.ShapeDtypeStruct((members - 1, WIN, width), BF)]
        + [pltpu.VMEM(x.shape, BF) for x in (w_key, w_value)],
        in_specs=[VMEM] + [HBM] * 4,
        out_specs=[VMEM] * 6,
        scratch_shapes=[
            pltpu.VMEM(states.shape, BF),
            pltpu.VMEM(noise.shape, F32),
            pltpu.VMEM(w_query.shape, BF),
            pltpu.SemaphoreType.DMA((4,)),
        ],
        compiler_params=params(20),
        cost_estimate=pl.CostEstimate(
            flops=6 * members * rows * width * width, bytes_accessed=8 * 2**20, transcendentals=0
        ),
        name="own_qkv",
    )(states, *[pltpu.with_memory_space_constraint(x, pltpu.HBM) for x in (noise, w_query, w_key, w_value)])


def attend_kernel(
    m, states, noise, inner, outer, query, keys, values, w_key, w_value, w_out, w_decode, earlier,
    forecast, w_both, halo_k, halo_v, kk, vv, mixed, bad,
):
    members, rows, width = states.shape
    pairs = width // SUB
    subs = rows // SUB
    pad = WIN // SUB
    span = 2 * pad + 1
    total = subs + 2 * pad
    lane = lax.broadcasted_iota(jnp.int32, (SUB, SUB), 1)
    row = lax.broadcasted_iota(jnp.int32, (SUB, SUB), 0)
    left = lane < SUB // 2
    zero = jnp.zeros((SUB, SUB), BF)
    one = jnp.ones((SUB, SUB), BF)
    place = lax.axis_index("space")
    even = place % 2 == 0
    starts = place == 0
    ends = place == lax.axis_size("space") - 1

    def absent(j):
        return starts if j < pad else ends

    def outside(j):
        return j < pad or j >= pad + subs

    for u in range(UNROLL):
        for j in range(total):
            unit = jnp.where(absent(j), zero, one) if outside(j) else one
            at = 2 * SUB * j
            vv[u, at : at + SUB, SUB:] = jnp.where(left, unit, zero)
            vv[u, at + SUB : at + 2 * SUB, SUB:] = jnp.where(left, zero, unit)

    def source(m, inner, halo, j, c):
        if j < pad:
            return halo[j * SUB : (j + 1) * SUB, c]
        if j < pad + subs:
            return inner[m, (j - pad) * SUB : (j - pad + 1) * SUB, c]
        return halo[(j - subs) * SUB : (j - subs + 1) * SUB, c]

    def pack(m, u, pair):
        c = pl.ds(pl.multiple_of(pair * SUB, SUB), SUB)
        for j in range(total):
            at = 2 * SUB * j
            key = source(m, keys, halo_k, j, c)
            value = source(m, values, halo_v, j, c)
            if outside(j):
                value = jnp.where(absent(j), zero, value)
            kk[u, at : at + SUB] = jnp.where(left, key, zero)
            kk[u, at + SUB : at + 2 * SUB] = jnp.where(left, zero, key)
            vv[u, at : at + SUB, :SUB] = jnp.where(left, value, zero)
            vv[u, at + SUB : at + 2 * SUB, :SUB] = jnp.where(left, zero, value)

    def masked(s, j):
        if j == 0:
            return jnp.where(lane >= row, s, -1e30)
        if j == span - 1:
            return jnp.where(lane <= row, s, -1e30)
        return s

    def block(m, u, pair, a):
        c = pl.ds(pl.multiple_of(pair * SUB, SUB), SUB)
        at = slice(2 * SUB * a, 2 * SUB * (a + span))
        s = lax.dot_general(
            query[m, a * SUB : (a + 1) * SUB, c], kk[u, at], NT, preferred_element_type=F32
        )
        parts = []
        for j in range(2 * span):
            parts.append(jnp.exp2(masked(s[:, j * SUB : (j + 1) * SUB] * LOG2E, j // 2)).astype(BF))
        o = jnp.dot(jnp.concatenate(parts, axis=1), vv[u, at], preferred_element_type=F32)
        norms = o[:, SUB:]
        mixed[a * SUB : (a + 1) * SUB, c] = (o[:, :SUB] / norms).astype(BF)
        bad[...] = jnp.where((norms > LOW) & (norms < HIGH), bad[...], 1.0)

    def safe_block(m, pair, a):
        c = pl.ds(pl.multiple_of(pair * SUB, SUB), SUB)
        q = query[m, a * SUB : (a + 1) * SUB, c]
        outs = []
        for side in range(2):
            mine = left if side == 0 else ~left
            scores, vals = [], []
            for j in range(a, a + span):
                key = source(m, keys, halo_k, j, c)
                own = jnp.where(mine, q, zero)
                s = lax.dot_general(own, key, NT, preferred_element_type=F32)
                s = masked(s * LOG2E, j - a)
                if outside(j):
                    s = jnp.where(absent(j), -1e30, s)
                scores.append(s)
                vals.append(source(m, values, halo_v, j, c))
            s = jnp.concatenate(scores, axis=1)
            p = jnp.exp2(s - jnp.max(s, axis=-1, keepdims=True))
            norms = jnp.sum(p, axis=-1, keepdims=True)
            outs.append(
                jnp.dot(
                    (p / norms).astype(BF),
                    jnp.concatenate(vals, axis=0),
                    preferred_element_type=F32,
                )
            )
        mixed[a * SUB : (a + 1) * SUB, c] = jnp.where(left, outs[0], outs[1]).astype(BF)

    shift = noise[m : m + 1]
    for side in range(2):
        x = normed(jnp.where(even == (side == 0), outer[...], inner[m]), shift)
        at = slice(side * WIN, (side + 1) * WIN)
        halo_k[at] = jnp.dot(x, w_key[...], preferred_element_type=F32).astype(BF)
        halo_v[at] = jnp.dot(x, w_value[...], preferred_element_type=F32).astype(BF)
    bad[...] = jnp.zeros_like(bad)

    lanes = w_decode.shape[1]
    if m == 0:
        product = jnp.dot(w_out[...], w_decode[...], preferred_element_type=F32)
        w_both[:, :lanes], w_both[:, lanes:] = split(product, 2)
    else:
        w_both[...] = earlier[0][...]
        for i in range(m):
            forecast[:, i] = earlier[1][:, i]

    def heads(i, _):
        for u in range(UNROLL):
            pack(m, u, i * UNROLL + u)
        for u in range(UNROLL):
            for a in range(subs):
                block(m, u, i * UNROLL + u, a)
        return 0

    lax.fori_loop(0, pairs // UNROLL, heads, 0)

    @pl.when(jnp.max(bad[...]) > 0.0)
    def _():
        def again(pair, _):
            for a in range(subs):
                safe_block(m, pair, a)
            return 0

        lax.fori_loop(0, pairs, again, 0)

    constant = jnp.dot(
        jnp.concatenate([jnp.broadcast_to(x, (8, width)) for x in split(shift, 3)], axis=0),
        w_decode[...],
        preferred_element_type=F32,
    )
    constant = constant[0:1] + constant[8:9] + constant[16:17]
    for i in range(rows // 256):
        at = slice(i * 256, (i + 1) * 256)
        out = jnp.dot(mixed[at], w_both[...], preferred_element_type=F32)
        out = out[:, :lanes] + out[:, lanes:] + constant
        out = out + jnp.dot(states[m, at], w_decode[...], preferred_element_type=F32)
        share = rows // forecast.shape[0]
        each = 256 // share
        forecast[i * each : (i + 1) * each, m] = out.astype(BF).reshape(each, share, -1)


def attend(m, states, noise, inner, outer, query, keys, values, w_key, w_value, w_out, w_decode, shares, earlier):
    members, rows, width = states.shape
    held = 2 * WIN + rows
    lanes = w_decode.shape[1]
    taken = [] if earlier is None else list(earlier)

    def kernel(*refs):
        ins, rest = refs[:11], refs[11:]
        attend_kernel(m, *ins, rest[: len(taken)], *rest[len(taken) :])

    return pl.pallas_call(
        kernel,
        out_shape=[
            jax.ShapeDtypeStruct((shares, members, rows // shares, lanes), BF),
            jax.ShapeDtypeStruct((width, 2 * lanes), BF),
        ],
        in_specs=[VMEM] * (11 + len(taken)),
        out_specs=[VMEM] * 2,
        scratch_shapes=[
            pltpu.VMEM((2 * WIN, width), BF),
            pltpu.VMEM((2 * WIN, width), BF),
            pltpu.VMEM((UNROLL, 2 * held, SUB), BF),
            pltpu.VMEM((UNROLL, 2 * held, 2 * SUB), BF),
            pltpu.VMEM((rows, width), BF),
            pltpu.VMEM((SUB, SUB), F32),
        ],
        compiler_params=params(24),
        cost_estimate=pl.CostEstimate(
            flops=12 * rows * width * width,
            bytes_accessed=8 * 2**20,
            transcendentals=rows * HEADS * 640,
        ),
        name="window_attention",
    )(states, noise, inner, outer, query, keys, values, w_key, w_value, w_out, w_decode, *taken)


def crps_kernel(gathered, target, grad):
    groups, local, share, lanes = gathered.shape
    members = groups * local
    first = lax.axis_index("ens") * share

    def piece(i, total):
        at = pl.ds(pl.multiple_of(i * 16, 16), 16)
        out = []
        for half in range(2):
            cut = slice(half * 8, half * 8 + 8)
            goal = target[pl.ds(pl.multiple_of(first + i * 16 + half * 8, 8), 8)]
            pred = [gathered[m // local, m % local, at].astype(F32)[cut] for m in range(members)]
            slopes = [None] * members
            spread = jnp.zeros_like(goal)
            pull = []
            for a in range(members):
                delta = pred[a] - goal
                square = delta * delta + SMOOTH * SMOOTH
                inv = lax.rsqrt(square)
                pull.append(delta * inv)
                total = total + square * inv
                for b in range(a + 1, members):
                    delta = pred[a] - pred[b]
                    square = delta * delta + SMOOTH * SMOOTH
                    inv = lax.rsqrt(square)
                    f = delta * inv
                    spread = spread + square * inv
                    slopes[a] = f if slopes[a] is None else slopes[a] + f
                    slopes[b] = -f if slopes[b] is None else slopes[b] - f
            total = total - (2.0 * spread + members * SMOOTH) / (2 * (members - 1))
            out.append([pull[a] - slopes[a] / (members - 1) for a in range(members)])
        for m in range(members):
            to = pl.ds(pl.multiple_of(m % local * share + i * 16, 16), 16)
            grad[m // local, to] = jnp.concatenate([out[0][m], out[1][m]], 0).astype(BF)
        return total

    total = lax.fori_loop(0, share // 16, piece, jnp.zeros((8, lanes), F32))
    terms = split(jnp.sum(total, axis=0, keepdims=True), 3)
    row = lax.broadcasted_iota(jnp.int32, (TAIL, lanes), 0)
    tail = jnp.zeros((TAIL, lanes), F32)
    for i, term in enumerate(terms):
        tail = jnp.where(row == i, term.astype(F32), tail)
    for i in range(groups):
        grad[i, local * share :] = tail.astype(BF)


def crps(gathered, target):
    groups, local, share, lanes = gathered.shape
    return pl.pallas_call(
        crps_kernel,
        out_shape=jax.ShapeDtypeStruct((groups, local * share + TAIL, lanes), BF),
        in_specs=[VMEM, VMEM],
        out_specs=VMEM,
        compiler_params=params(8),
        name="fair_crps",
    )(gathered, target)


def back_kernel(members, slopes, w_decode, grad):
    shares, held, lanes = slopes.shape
    share = (held - TAIL) // members
    steps = pl.num_programs(0) // members
    each = shares // steps
    step = pl.program_id(0)
    at = pl.ds(pl.multiple_of(step // steps * share, 16), share)
    rows = slopes[pl.ds(step % steps * each, each), at].reshape(each * share, lanes)
    grad[0] = lax.dot_general(rows, w_decode[...], NT, preferred_element_type=F32).astype(BF)


def back(slopes, w_decode, members):
    shares, held, lanes = slopes.shape
    share = (held - TAIL) // members
    width = w_decode.shape[0]
    steps = 2
    rows = shares * share
    return pl.pallas_call(
        functools.partial(back_kernel, members),
        grid=(members * steps,),
        out_shape=jax.ShapeDtypeStruct((members, rows, width), BF),
        in_specs=[
            pl.BlockSpec(slopes.shape, lambda i: (0, 0, 0)),
            pl.BlockSpec(w_decode.shape, lambda i: (0, 0)),
        ],
        out_specs=pl.BlockSpec((1, rows // steps, width), lambda i: (i // steps, i % steps, 0)),
        compiler_params=params(12),
        cost_estimate=pl.CostEstimate(
            flops=2 * members * rows * width * lanes, bytes_accessed=3 * 2**20, transcendentals=0
        ),
        name="state_grad",
    )(slopes, w_decode)


def body(states, member_noise, w_query, w_key, w_value, w_out, w_decode, target):
    members, rows, width = states.shape
    ens, space = lax.axis_size("ens"), lax.axis_size("space")
    cross = [(i, i + 1) for i in range(1, space - 1, 2)]
    chip = [(i, i + 1) for i in range(0, space, 2)]
    both = lambda pairs: pairs + [(j, i) for i, j in pairs]
    far, near = edges(states)
    outer = [lax.ppermute(far, "space", both(cross))]
    inner = lax.ppermute(near, "space", both(chip))
    query, keys, values, far, w_key, w_value = qkv(
        states, member_noise, w_query, w_key, w_value
    )
    outer += [lax.ppermute(far[m], "space", both(cross)) for m in range(members - 1)]
    done = None
    for m in range(members):
        done = attend(
            m, states, member_noise, inner, outer[m], query, keys, values,
            w_key, w_value, w_out, w_decode, ens, done and (done[1], done[0]),
        )
    gathered = lax.all_to_all(done[0], "ens", 0, 0)
    slopes = lax.all_to_all(crps(gathered, target), "ens", 0, 0)
    held = slopes.shape[1] - TAIL
    part = jnp.sum(slopes[:, held : held + 3].astype(F32), axis=(0, 1))
    parts = lax.all_to_all(jnp.broadcast_to(part, (space, 1, part.shape[0])), "space", 0, 0)
    loss = jnp.sum(parts) / (members * ens * rows * space * w_decode.shape[1])
    return back(slopes, w_decode, members), loss


def solution(mesh):
    in_specs = (P("ens", "space", None), P("ens", None), P(), P(), P(), P(), P(), P("space", None))
    out_specs = (P("ens", "space", None), P())
    return jax.shard_map(body, mesh=mesh, in_specs=in_specs, out_specs=out_specs, check_vma=False)
```

```python
import functools
import math

import jax
import jax.numpy as jnp
from jax import lax
from jax.experimental import pallas as pl
from jax.experimental.pallas import tpu as pltpu
from jax.sharding import PartitionSpec as P

HEADS = 16
WIN = 256
SMOOTH = 0.25
EPS = 1e-5
SUB = 128
UNROLL = 4
TAIL = 16
LOW, HIGH = 2.0**-80, 2.0**100
BF, F32 = jnp.bfloat16, jnp.float32
VMEM = pl.BlockSpec(memory_space=pltpu.VMEM)
HBM = pl.BlockSpec(memory_space=pltpu.HBM)
NT = (((1,), (1,)), ((), ()))


def params(mib):
    return pltpu.CompilerParams(vmem_limit_bytes=mib * 2**20)


def normed(rows, noise):
    hidden = rows.astype(F32) + noise
    return (hidden * lax.rsqrt(jnp.mean(hidden * hidden, axis=-1, keepdims=True) + EPS)).astype(BF)


def split(x, terms):
    parts = []
    for _ in range(terms):
        parts.append(x.astype(BF))
        x = x - parts[-1].astype(F32)
    return parts


def edges_kernel(states, noise, w_query, far, near, shift, held_query, sems):
    rows = states.shape[1]
    even = lax.axis_index("space") % 2 == 0
    first, last = pl.ds(0, WIN), pl.ds(rows - WIN, WIN)

    def move(out, back):
        copies = [
            pltpu.make_async_copy(states.at[:, out], far, sems.at[0]),
            pltpu.make_async_copy(states.at[:, back], near, sems.at[1]),
            pltpu.make_async_copy(noise, shift, sems.at[2]),
            pltpu.make_async_copy(w_query, held_query, sems.at[3]),
        ]
        for copy in copies:
            copy.start()
        for copy in copies:
            copy.wait()

    @pl.when(even)
    def _():
        move(first, last)

    @pl.when(~even)
    def _():
        move(last, first)


def edges(states, noise, w_query):
    members, _, width = states.shape
    return pl.pallas_call(
        edges_kernel,
        out_shape=[
            jax.ShapeDtypeStruct((members, WIN, width), BF),
            jax.ShapeDtypeStruct((members, WIN, width), BF),
            pltpu.VMEM(noise.shape, F32),
            pltpu.VMEM(w_query.shape, BF),
        ],
        in_specs=[HBM] * 3,
        out_specs=[VMEM] * 4,
        scratch_shapes=[pltpu.SemaphoreType.DMA((4,))],
        compiler_params=params(4),
        name="edges",
    )(*[pltpu.with_memory_space_constraint(x, pltpu.HBM) for x in (states, noise, w_query)])


def qkv_kernel(
    states, noise, w_query, w_key, w_value, query, keys, values, held_key, held_value,
    norm, sems,
):
    members, rows, width = states.shape
    scale = 1.0 / math.sqrt(width // HEADS)
    step = 256
    pieces = [(m, pl.ds(i * step, step)) for m in range(members) for i in range(rows // step)]
    moves = [(w_key, held_key), (w_value, held_value)]
    copies = [pltpu.make_async_copy(a, b, sems.at[i]) for i, (a, b) in enumerate(moves)]
    for copy in copies:
        copy.start()
    for m, at in pieces[:1]:
        norm[m, at] = normed(states[m, at], noise[m : m + 1])
    for i, (m, at) in enumerate(pieces):
        x = norm[m, at]
        query[m, at] = (jnp.dot(x, w_query[...], preferred_element_type=F32) * scale).astype(BF)
        for later, part in pieces[i + 1 : i + 2]:
            norm[later, part] = normed(states[later, part], noise[later : later + 1])
    copies[0].wait()
    for m, at in pieces:
        keys[m, at] = jnp.dot(norm[m, at], held_key[...], preferred_element_type=F32).astype(BF)
    copies[1].wait()
    for m, at in pieces:
        values[m, at] = jnp.dot(norm[m, at], held_value[...], preferred_element_type=F32).astype(BF)


def qkv(states, noise, w_query, w_key, w_value):
    members, rows, width = states.shape
    return pl.pallas_call(
        qkv_kernel,
        out_shape=[jax.ShapeDtypeStruct(states.shape, BF)] * 3
        + [pltpu.VMEM(x.shape, BF) for x in (w_key, w_value)],
        in_specs=[VMEM] * 3 + [HBM] * 2,
        out_specs=[VMEM] * 5,
        scratch_shapes=[
            pltpu.VMEM(states.shape, BF),
            pltpu.SemaphoreType.DMA((2,)),
        ],
        compiler_params=params(20),
        cost_estimate=pl.CostEstimate(
            flops=6 * members * rows * width * width, bytes_accessed=8 * 2**20, transcendentals=0
        ),
        name="own_qkv",
    )(states, noise, w_query, *[pltpu.with_memory_space_constraint(x, pltpu.HBM) for x in (w_key, w_value)])


def attend_kernel(
    m, states, noise, inner, outer, query, keys, values, w_key, w_value, w_out, w_decode, earlier,
    w_both, forecast, halo_k, halo_v, kk, vv, mixed, bad, base,
):
    members, rows, width = states.shape
    pairs = width // SUB
    subs = rows // SUB
    pad = WIN // SUB
    span = 2 * pad + 1
    total = subs + 2 * pad
    lane = lax.broadcasted_iota(jnp.int32, (SUB, SUB), 1)
    row = lax.broadcasted_iota(jnp.int32, (SUB, SUB), 0)
    left = lane < SUB // 2
    zero = jnp.zeros((SUB, SUB), BF)
    one = jnp.ones((SUB, SUB), BF)
    place = lax.axis_index("space")
    even = place % 2 == 0
    starts = place == 0
    ends = place == lax.axis_size("space") - 1

    def absent(j):
        return starts if j < pad else ends

    def outside(j):
        return j < pad or j >= pad + subs

    for u in range(UNROLL):
        for j in range(total):
            unit = jnp.where(absent(j), zero, one) if outside(j) else one
            at = 2 * SUB * j
            vv[u, at : at + SUB, SUB:] = jnp.where(left, unit, zero)
            vv[u, at + SUB : at + 2 * SUB, SUB:] = jnp.where(left, zero, unit)

    def source(m, inner, halo, j, c):
        if j < pad:
            return halo[j * SUB : (j + 1) * SUB, c]
        if j < pad + subs:
            return inner[m, (j - pad) * SUB : (j - pad + 1) * SUB, c]
        return halo[(j - subs) * SUB : (j - subs + 1) * SUB, c]

    def pack(m, u, pair):
        c = pl.ds(pl.multiple_of(pair * SUB, SUB), SUB)
        for j in range(total):
            at = 2 * SUB * j
            key = source(m, keys, halo_k, j, c)
            value = source(m, values, halo_v, j, c)
            if outside(j):
                value = jnp.where(absent(j), zero, value)
            kk[u, at : at + SUB] = jnp.where(left, key, zero)
            kk[u, at + SUB : at + 2 * SUB] = jnp.where(left, zero, key)
            vv[u, at : at + SUB, :SUB] = jnp.where(left, value, zero)
            vv[u, at + SUB : at + 2 * SUB, :SUB] = jnp.where(left, zero, value)

    def masked(s, j):
        if j == 0:
            return jnp.where(lane >= row, s, -1e30)
        if j == span - 1:
            return jnp.where(lane <= row, s, -1e30)
        return s

    def block(m, u, pair, a):
        c = pl.ds(pl.multiple_of(pair * SUB, SUB), SUB)
        at = slice(2 * SUB * a, 2 * SUB * (a + span))
        s = lax.dot_general(
            query[m, a * SUB : (a + 1) * SUB, c], kk[u, at], NT, preferred_element_type=F32
        )
        parts = []
        for j in range(2 * span):
            parts.append(jnp.exp(masked(s[:, j * SUB : (j + 1) * SUB], j // 2)).astype(BF))
        o = jnp.dot(jnp.concatenate(parts, axis=1), vv[u, at], preferred_element_type=F32)
        norms = o[:, SUB:]
        mixed[a * SUB : (a + 1) * SUB, c] = (o[:, :SUB] / norms).astype(BF)
        bad[...] = jnp.where((norms > LOW) & (norms < HIGH), bad[...], 1.0)

    def safe_block(m, pair, a):
        c = pl.ds(pl.multiple_of(pair * SUB, SUB), SUB)
        q = query[m, a * SUB : (a + 1) * SUB, c]
        outs = []
        for side in range(2):
            mine = left if side == 0 else ~left
            scores, vals = [], []
            for j in range(a, a + span):
                key = source(m, keys, halo_k, j, c)
                own = jnp.where(mine, q, zero)
                s = lax.dot_general(own, key, NT, preferred_element_type=F32)
                s = masked(s, j - a)
                if outside(j):
                    s = jnp.where(absent(j), -1e30, s)
                scores.append(s)
                vals.append(source(m, values, halo_v, j, c))
            s = jnp.concatenate(scores, axis=1)
            p = jnp.exp(s - jnp.max(s, axis=-1, keepdims=True))
            norms = jnp.sum(p, axis=-1, keepdims=True)
            outs.append(
                jnp.dot(
                    (p / norms).astype(BF),
                    jnp.concatenate(vals, axis=0),
                    preferred_element_type=F32,
                )
            )
        mixed[a * SUB : (a + 1) * SUB, c] = jnp.where(left, outs[0], outs[1]).astype(BF)

    shift = noise[m : m + 1]
    for side in range(2):
        x = normed(jnp.where(even == (side == 0), outer[...], inner[m]), shift)
        at = slice(side * WIN, (side + 1) * WIN)
        halo_k[at] = jnp.dot(x, w_key[...], preferred_element_type=F32).astype(BF)
        halo_v[at] = jnp.dot(x, w_value[...], preferred_element_type=F32).astype(BF)
    bad[...] = jnp.zeros_like(bad)

    lanes = w_decode.shape[1]
    if m == 0:
        product = jnp.dot(w_out[...], w_decode[...], preferred_element_type=F32)
        w_both[:, :lanes], w_both[:, lanes:] = split(product, 2)
    else:
        for i in range(m):
            forecast[:, i] = earlier[:, i]

    constant = jnp.dot(
        jnp.concatenate([jnp.broadcast_to(x, (8, width)) for x in split(shift, 3)], axis=0),
        w_decode[...],
        preferred_element_type=F32,
    )
    constant = constant[0:1] + constant[8:9] + constant[16:17]
    base[...] = jnp.dot(states[m], w_decode[...], preferred_element_type=F32) + constant

    def heads(i, _):
        for u in range(UNROLL):
            pack(m, u, i * UNROLL + u)
        for u in range(UNROLL):
            for a in range(subs):
                block(m, u, i * UNROLL + u, a)
        return 0

    def finish():
        share = rows // forecast.shape[0]
        for i in range(rows // 256):
            at = slice(i * 256, (i + 1) * 256)
            out = jnp.dot(mixed[at], w_both[...], preferred_element_type=F32)
            out = out[:, :lanes] + out[:, lanes:] + base[at]
            each = 256 // share
            forecast[i * each : (i + 1) * each, m] = out.astype(BF).reshape(each, share, -1)

    lax.fori_loop(0, pairs // UNROLL, heads, 0)
    finish()

    @pl.when(jnp.max(bad[...]) > 0.0)
    def _():
        def again(pair, _):
            for a in range(subs):
                safe_block(m, pair, a)
            return 0

        lax.fori_loop(0, pairs, again, 0)
        finish()


def attend(m, states, noise, inner, outer, query, keys, values, w_key, w_value, w_out, w_decode, shares, earlier):
    members, rows, width = states.shape
    held = 2 * WIN + rows
    lanes = w_decode.shape[1]
    ready = jax.ShapeDtypeStruct((shares, members, rows // shares, lanes), BF)
    product = jax.ShapeDtypeStruct((width, 2 * lanes), BF)
    taken = [] if earlier is None else list(earlier)

    def kernel(*refs):
        ins, rest = refs[:11], refs[11:]
        if taken:
            before, w_both, forecast = rest[:3]
        else:
            before, w_both, forecast = None, rest[0], rest[1]
        attend_kernel(m, *ins, before, w_both, forecast, *rest[2 + len(taken) // 2 :])

    return pl.pallas_call(
        kernel,
        out_shape=[ready] if taken else [product, ready],
        in_specs=[VMEM] * (11 + len(taken)),
        out_specs=[VMEM] * (1 if taken else 2),
        scratch_shapes=[
            pltpu.VMEM((2 * WIN, width), BF),
            pltpu.VMEM((2 * WIN, width), BF),
            pltpu.VMEM((UNROLL, 2 * held, SUB), BF),
            pltpu.VMEM((UNROLL, 2 * held, 2 * SUB), BF),
            pltpu.VMEM((rows, width), BF),
            pltpu.VMEM((SUB, SUB), F32),
            pltpu.VMEM((rows, lanes), F32),
        ],
        compiler_params=params(24),
        cost_estimate=pl.CostEstimate(
            flops=12 * rows * width * width,
            bytes_accessed=8 * 2**20,
            transcendentals=rows * HEADS * 640,
        ),
        name="window_attention",
    )(states, noise, inner, outer, query, keys, values, w_key, w_value, w_out, w_decode, *taken)


def crps_kernel(count, gathered, target, grad):
    groups, local, share, lanes = gathered.shape
    members = groups * local
    first = lax.axis_index("ens") * share

    def piece(i, total):
        at = pl.ds(pl.multiple_of(i * 16, 16), 16)
        out = []
        for half in range(2):
            cut = slice(half * 8, half * 8 + 8)
            goal = target[pl.ds(pl.multiple_of(first + i * 16 + half * 8, 8), 8)]
            pred = [gathered[m // local, m % local, at].astype(F32)[cut] for m in range(members)]
            slopes = [None] * members
            spread = jnp.zeros_like(goal)
            pull = []
            for a in range(members):
                delta = pred[a] - goal
                square = delta * delta + SMOOTH * SMOOTH
                inv = lax.rsqrt(square)
                pull.append(delta * inv)
                total = total + square * inv
                for b in range(a + 1, members):
                    delta = pred[a] - pred[b]
                    square = delta * delta + SMOOTH * SMOOTH
                    inv = lax.rsqrt(square)
                    f = delta * inv
                    spread = spread + square * inv
                    slopes[a] = f if slopes[a] is None else slopes[a] + f
                    slopes[b] = -f if slopes[b] is None else slopes[b] - f
            total = total - (2.0 * spread + members * SMOOTH) / (2 * (members - 1))
            out.append([pull[a] - slopes[a] / (members - 1) for a in range(members)])
        for m in range(members):
            to = pl.ds(pl.multiple_of(m % local * share + i * 16, 16), 16)
            grad[m // local, to] = jnp.concatenate([out[0][m], out[1][m]], 0).astype(BF)
        return total

    total = lax.fori_loop(0, share // 16, piece, jnp.zeros((8, lanes), F32))
    terms = split(jnp.sum(total, axis=0, keepdims=True) * (1.0 / count), 3)
    row = lax.broadcasted_iota(jnp.int32, (TAIL, lanes), 0)
    tail = jnp.zeros((TAIL, lanes), F32)
    for i, term in enumerate(terms):
        tail = jnp.where(row == i, term.astype(F32), tail)
    for i in range(groups):
        grad[i, local * share :] = tail.astype(BF)


def crps(gathered, target, count):
    groups, local, share, lanes = gathered.shape
    return pl.pallas_call(
        functools.partial(crps_kernel, count),
        out_shape=jax.ShapeDtypeStruct((groups, local * share + TAIL, lanes), BF),
        in_specs=[VMEM, VMEM],
        out_specs=VMEM,
        compiler_params=params(8),
        name="fair_crps",
    )(gathered, target)


def back_kernel(members, slopes, w_decode, grad):
    shares, held, lanes = slopes.shape
    share = (held - TAIL) // members
    steps = pl.num_programs(0) // members
    each = shares // steps
    step = pl.program_id(0)
    at = pl.ds(pl.multiple_of(step // steps * share, 16), share)
    rows = slopes[pl.ds(step % steps * each, each), at].reshape(each * share, lanes)
    grad[0] = lax.dot_general(rows, w_decode[...], NT, preferred_element_type=F32).astype(BF)


def back(slopes, w_decode, members):
    shares, held, lanes = slopes.shape
    share = (held - TAIL) // members
    width = w_decode.shape[0]
    steps = 2
    rows = shares * share
    return pl.pallas_call(
        functools.partial(back_kernel, members),
        grid=(members * steps,),
        out_shape=jax.ShapeDtypeStruct((members, rows, width), BF),
        in_specs=[
            pl.BlockSpec(slopes.shape, lambda i: (0, 0, 0)),
            pl.BlockSpec(w_decode.shape, lambda i: (0, 0)),
        ],
        out_specs=pl.BlockSpec((1, rows // steps, width), lambda i: (i // steps, i % steps, 0)),
        compiler_params=params(12),
        cost_estimate=pl.CostEstimate(
            flops=2 * members * rows * width * lanes, bytes_accessed=3 * 2**20, transcendentals=0
        ),
        name="state_grad",
    )(slopes, w_decode)


def body(states, member_noise, w_query, w_key, w_value, w_out, w_decode, target):
    members, rows, width = states.shape
    ens, space = lax.axis_size("ens"), lax.axis_size("space")
    cross = [(i, i + 1) for i in range(1, space - 1, 2)]
    chip = [(i, i + 1) for i in range(0, space, 2)]
    both = lambda pairs: pairs + [(j, i) for i, j in pairs]
    far, near, member_noise, w_query = edges(states, member_noise, w_query)
    outer = [lax.ppermute(far[m], "space", both(cross)) for m in range(members)]
    inner = lax.ppermute(near, "space", both(chip))
    query, keys, values, w_key, w_value = qkv(
        states, member_noise, w_query, w_key, w_value
    )
    taken = None
    for m in range(members):
        done = attend(
            m, states, member_noise, inner, outer[m], query, keys, values,
            w_key, w_value, w_out, w_decode, ens, taken,
        )
        product = product if m else done[0]
        taken = (done[-1], product)
    gathered = lax.all_to_all(done[-1], "ens", 0, 0)
    count = members * ens * rows * space * w_decode.shape[1]
    slopes = lax.all_to_all(crps(gathered, target, count), "ens", 0, 0)
    held = slopes.shape[1] - TAIL
    part = jnp.sum(slopes[:, held : held + 3].astype(F32), axis=(0, 1))
    parts = lax.all_to_all(jnp.broadcast_to(part, (space, 1, part.shape[0])), "space", 0, 0)
    return back(slopes, w_decode, members), jnp.sum(parts)


def solution(mesh):
    in_specs = (P("ens", "space", None), P("ens", None), P(), P(), P(), P(), P(), P("space", None))
    out_specs = (P("ens", "space", None), P())
    return jax.shard_map(body, mesh=mesh, in_specs=in_specs, out_specs=out_specs, check_vma=False)
```

```python
import functools
import math
import types

import jax
import jax.numpy as jnp
from jax import lax
from jax.experimental import pallas as pl
from jax.experimental.pallas import tpu as pltpu
from jax.sharding import PartitionSpec as P

HEADS = 16
WIN = 256
SMOOTH = 0.25
EPS = 1e-5
SUB = 128
UNROLL = {"own": 8, "halo": 8, "all": 8}
AHEAD = {"own": 1, "halo": 2, "all": 0}
CHUNK = {"own": 4, "halo": 2, "all": 5}
TAIL = 16
LOW, HIGH = 2.0**-80, 2.0**100
BF, F32 = jnp.bfloat16, jnp.float32
VMEM = pl.BlockSpec(memory_space=pltpu.VMEM)
HBM = pl.BlockSpec(memory_space=pltpu.HBM)
NT = (((1,), (1,)), ((), ()))


def params(mib):
    return pltpu.CompilerParams(vmem_limit_bytes=mib * 2**20)


def normed(rows, noise):
    hidden = rows.astype(F32) + noise
    return (hidden * lax.rsqrt(jnp.mean(hidden * hidden, axis=-1, keepdims=True) + EPS)).astype(BF)


def split(x, terms):
    parts = []
    for _ in range(terms):
        parts.append(x.astype(BF))
        x = x - parts[-1].astype(F32)
    return parts


def edges_kernel(states, noise, w_query, far, near, shift, held_query, sems):
    rows = states.shape[1]
    even = lax.axis_index("space") % 2 == 0
    first, last = pl.ds(0, WIN), pl.ds(rows - WIN, WIN)

    def move(out, back):
        copies = [
            pltpu.make_async_copy(states.at[:, out], far, sems.at[0]),
            pltpu.make_async_copy(states.at[:, back], near, sems.at[1]),
            pltpu.make_async_copy(noise, shift, sems.at[2]),
            pltpu.make_async_copy(w_query, held_query, sems.at[3]),
        ]
        for copy in copies:
            copy.start()
        for copy in copies:
            copy.wait()

    @pl.when(even)
    def _():
        move(first, last)

    @pl.when(~even)
    def _():
        move(last, first)


def edges(states, noise, w_query):
    members, _, width = states.shape
    return pl.pallas_call(
        edges_kernel,
        out_shape=[
            jax.ShapeDtypeStruct((members, WIN, width), BF),
            jax.ShapeDtypeStruct((members, WIN, width), BF),
            pltpu.VMEM(noise.shape, F32),
            pltpu.VMEM(w_query.shape, BF),
        ],
        in_specs=[HBM] * 3,
        out_specs=[VMEM] * 4,
        scratch_shapes=[pltpu.SemaphoreType.DMA((4,))],
        compiler_params=params(4),
        name="edges",
    )(*[pltpu.with_memory_space_constraint(x, pltpu.HBM) for x in (states, noise, w_query)])


def qkv_kernel(
    states, noise, w_query, w_key, w_value, query, keys, values, held_key, held_value,
    norm, sems,
):
    members, rows, width = states.shape
    scale = 1.0 / math.sqrt(width // HEADS)
    step = 256
    pieces = [(m, pl.ds(i * step, step)) for m in range(members) for i in range(rows // step)]
    moves = [(w_key, held_key), (w_value, held_value)]
    copies = [pltpu.make_async_copy(a, b, sems.at[i]) for i, (a, b) in enumerate(moves)]
    for copy in copies:
        copy.start()
    for m, at in pieces[:1]:
        norm[m, at] = normed(states[m, at], noise[m : m + 1])
    for i, (m, at) in enumerate(pieces):
        x = norm[m, at]
        query[m, at] = (jnp.dot(x, w_query[...], preferred_element_type=F32) * scale).astype(BF)
        for later, part in pieces[i + 1 : i + 2]:
            norm[later, part] = normed(states[later, part], noise[later : later + 1])
    copies[0].wait()
    for m, at in pieces:
        keys[m, at] = jnp.dot(norm[m, at], held_key[...], preferred_element_type=F32).astype(BF)
    copies[1].wait()
    for m, at in pieces:
        values[m, at] = jnp.dot(norm[m, at], held_value[...], preferred_element_type=F32).astype(BF)


def qkv(states, noise, w_query, w_key, w_value):
    members, rows, width = states.shape
    return pl.pallas_call(
        qkv_kernel,
        out_shape=[jax.ShapeDtypeStruct(states.shape, BF)] * 3
        + [pltpu.VMEM(x.shape, BF) for x in (w_key, w_value)],
        in_specs=[VMEM] * 3 + [HBM] * 2,
        out_specs=[VMEM] * 5,
        scratch_shapes=[
            pltpu.VMEM(states.shape, BF),
            pltpu.SemaphoreType.DMA((2,)),
        ],
        compiler_params=params(20),
        cost_estimate=pl.CostEstimate(
            flops=6 * members * rows * width * width, bytes_accessed=8 * 2**20, transcendentals=0
        ),
        name="own_qkv",
    )(states, noise, w_query, *[pltpu.with_memory_space_constraint(x, pltpu.HBM) for x in (w_key, w_value)])


def attend_kernel(kind, m, names, *refs):
    r = types.SimpleNamespace(**dict(zip(names, refs)))
    query, keys, values = r.query, r.keys, r.values
    kk, vv = r.kk, r.vv
    unroll = UNROLL[kind]
    members, rows, width = query.shape
    pairs = width // SUB
    subs = rows // SUB
    pad = WIN // SUB
    span = 2 * pad + 1
    total = subs + 2 * pad
    inside = [j for j in range(total) if pad <= j < pad + subs]
    held = {"own": inside, "halo": [j for j in range(total) if j not in inside]}
    held = held.get(kind, list(range(total)))
    lane = lax.broadcasted_iota(jnp.int32, (SUB, SUB), 1)
    row = lax.broadcasted_iota(jnp.int32, (SUB, SUB), 0)
    left = lane < SUB // 2
    zero = jnp.zeros((SUB, SUB), BF)
    one = jnp.ones((SUB, SUB), BF)
    place = lax.axis_index("space")
    even = place % 2 == 0
    starts = place == 0
    ends = place == lax.axis_size("space") - 1

    def absent(j):
        return starts if j < pad else ends

    def outside(j):
        return j not in inside

    for u in range(unroll):
        for n, j in enumerate(held):
            unit = jnp.where(absent(j), zero, one) if outside(j) else one
            at = 2 * SUB * n
            vv[u, at : at + SUB, SUB:] = jnp.where(left, unit, zero)
            vv[u, at + SUB : at + 2 * SUB, SUB:] = jnp.where(left, zero, unit)

    def source(m, inner, halo, j, c):
        if j < pad:
            return halo[j * SUB : (j + 1) * SUB, c]
        if j < pad + subs:
            return inner[m, (j - pad) * SUB : (j - pad + 1) * SUB, c]
        return halo[(j - subs) * SUB : (j - subs + 1) * SUB, c]

    halo_k, halo_v = (None, None) if kind == "own" else (r.halo_k, r.halo_v)

    def pack(m, u, pair):
        c = pl.ds(pl.multiple_of(pair * SUB, SUB), SUB)
        for n, j in enumerate(held):
            at = 2 * SUB * n
            key = source(m, keys, halo_k, j, c)
            value = source(m, values, halo_v, j, c)
            if outside(j):
                value = jnp.where(absent(j), zero, value)
            kk[u, at : at + SUB] = jnp.where(left, key, zero)
            kk[u, at + SUB : at + 2 * SUB] = jnp.where(left, zero, key)
            vv[u, at : at + SUB, :SUB] = jnp.where(left, value, zero)
            vv[u, at + SUB : at + 2 * SUB, :SUB] = jnp.where(left, zero, value)

    def masked(s, j):
        if j == 0:
            return jnp.where(lane >= row, s, -1e30)
        if j == span - 1:
            return jnp.where(lane <= row, s, -1e30)
        return s

    def chunks(a):
        window = [j for j in range(a, a + span) if j in held]
        return [window[i : i + CHUNK[kind]] for i in range(0, len(window), CHUNK[kind])]

    def packed(window):
        first = held.index(window[0])
        return slice(2 * SUB * first, 2 * SUB * (first + len(window)))

    def weigh(m, u, pair, a, window):
        c = pl.ds(pl.multiple_of(pair * SUB, SUB), SUB)
        own = slice(a * SUB, (a + 1) * SUB)
        at = packed(window)
        s = lax.dot_general(query[m, own, c], kk[u, at], NT, preferred_element_type=F32)
        parts = []
        for n, j in enumerate(window):
            for k in range(2 * n, 2 * n + 2):
                parts.append(jnp.exp(masked(s[:, k * SUB : (k + 1) * SUB], j - a)).astype(BF))
        return jnp.concatenate(parts, axis=1)

    def mix(u, window, weights):
        return jnp.dot(weights, vv[u, packed(window)], preferred_element_type=F32)

    def store(pair, a, o):
        c = pl.ds(pl.multiple_of(pair * SUB, SUB), SUB)
        own = slice(a * SUB, (a + 1) * SUB)
        if kind == "own":
            r.partial[pair, own] = o
            return
        if kind == "halo":
            o = o + r.partial[pair, own]
        norms = o[:, SUB:]
        r.mixed[own, c] = (o[:, :SUB] / norms).astype(BF)
        r.bad[...] = jnp.where((norms > LOW) & (norms < HIGH), r.bad[...], 1.0)

    def safe_block(m, pair, a):
        c = pl.ds(pl.multiple_of(pair * SUB, SUB), SUB)
        q = query[m, a * SUB : (a + 1) * SUB, c]
        outs = []
        for side in range(2):
            mine = left if side == 0 else ~left
            scores, vals = [], []
            for j in range(a, a + span):
                key = source(m, keys, halo_k, j, c)
                own = jnp.where(mine, q, zero)
                s = lax.dot_general(own, key, NT, preferred_element_type=F32)
                s = masked(s, j - a)
                if outside(j):
                    s = jnp.where(absent(j), -1e30, s)
                scores.append(s)
                vals.append(source(m, values, halo_v, j, c))
            s = jnp.concatenate(scores, axis=1)
            p = jnp.exp(s - jnp.max(s, axis=-1, keepdims=True))
            norms = jnp.sum(p, axis=-1, keepdims=True)
            outs.append(
                jnp.dot(
                    (p / norms).astype(BF),
                    jnp.concatenate(vals, axis=0),
                    preferred_element_type=F32,
                )
            )
        r.mixed[a * SUB : (a + 1) * SUB, c] = jnp.where(left, outs[0], outs[1]).astype(BF)

    def heads(i, _):
        for u in range(unroll):
            pack(m, u, i * unroll + u)
        steps = [(u, a, w) for u in range(unroll) for a in range(subs) for w in chunks(a)]
        ready, sums = [], {}
        for n in range(len(steps) + AHEAD[kind]):
            if n < len(steps):
                u, a, window = steps[n]
                ready.append(weigh(m, u, i * unroll + u, a, window))
            if n >= AHEAD[kind]:
                u, a, window = steps[n - AHEAD[kind]]
                o = mix(u, window, ready[n - AHEAD[kind]])
                o = sums[u, a] + o if (u, a) in sums else o
                sums[u, a] = o
                if window == chunks(a)[-1]:
                    store(i * unroll + u, a, o)
        return 0

    shift = r.noise[m : m + 1]
    if kind != "halo":
        constant = jnp.dot(
            jnp.concatenate([jnp.broadcast_to(x, (8, width)) for x in split(shift, 3)], axis=0),
            r.w_decode[...],
            preferred_element_type=F32,
        )
        constant = constant[0:1] + constant[8:9] + constant[16:17]
        r.base[...] = constant + jnp.dot(
            r.states[m], r.w_decode[...], preferred_element_type=F32
        )
    if kind == "own":
        lanes = r.w_decode.shape[1]
        product = jnp.dot(r.w_out[...], r.w_decode[...], preferred_element_type=F32)
        r.w_both[:, :lanes], r.w_both[:, lanes:] = split(product, 2)
        lax.fori_loop(0, pairs // unroll, heads, 0)
        return

    for side in range(2):
        x = normed(jnp.where(even == (side == 0), r.outer[m], r.inner[m]), shift)
        at = slice(side * WIN, (side + 1) * WIN)
        halo_k[at] = jnp.dot(x, r.w_key[...], preferred_element_type=F32).astype(BF)
        halo_v[at] = jnp.dot(x, r.w_value[...], preferred_element_type=F32).astype(BF)
    r.bad[...] = jnp.zeros_like(r.bad)
    for i in range(m):
        r.forecast[:, i] = r.earlier[:, i]

    def finish():
        forecast = r.forecast
        lanes = forecast.shape[3]
        share = rows // forecast.shape[0]
        for i in range(rows // 256):
            at = slice(i * 256, (i + 1) * 256)
            out = jnp.dot(r.mixed[at], r.w_both[...], preferred_element_type=F32)
            out = out[:, :lanes] + out[:, lanes:] + r.base[at]
            each = 256 // share
            forecast[i * each : (i + 1) * each, m] = out.astype(BF).reshape(each, share, -1)

    lax.fori_loop(0, pairs // unroll, heads, 0)
    finish()

    @pl.when(jnp.max(r.bad[...]) > 0.0)
    def _():
        def again(pair, _):
            for a in range(subs):
                safe_block(m, pair, a)
            return 0

        lax.fori_loop(0, pairs, again, 0)
        finish()


def attend(kind, m, shares, **arrays):
    members, rows, width = arrays["query"].shape
    lanes = arrays["base" if kind == "halo" else "w_decode"].shape[1]
    keep = {"own": rows, "halo": 2 * WIN}.get(kind, 2 * WIN + rows)
    base = (rows, lanes)
    unroll = UNROLL[kind]
    ready = {"forecast": jax.ShapeDtypeStruct((shares, members, rows // shares, lanes), BF)}
    begun = {
        "partial": jax.ShapeDtypeStruct((width // SUB, rows, 2 * SUB), F32),
        "w_both": jax.ShapeDtypeStruct((width, 2 * lanes), BF),
        "base": jax.ShapeDtypeStruct(base, F32),
    }
    scratch = {
        "kk": pltpu.VMEM((unroll, 2 * keep, SUB), BF),
        "vv": pltpu.VMEM((unroll, 2 * keep, 2 * SUB), BF),
    }
    if kind != "own":
        scratch["halo_k"] = scratch["halo_v"] = pltpu.VMEM((2 * WIN, width), BF)
        scratch["mixed"] = pltpu.VMEM((rows, width), BF)
        scratch["bad"] = pltpu.VMEM((SUB, SUB), F32)
    if kind == "all":
        scratch["base"] = pltpu.VMEM(base, F32)
    outs = begun if kind == "own" else ready
    names = [*arrays, *outs, *scratch]
    done = pl.pallas_call(
        functools.partial(attend_kernel, kind, m, names),
        out_shape=list(outs.values()),
        in_specs=[VMEM] * len(arrays),
        out_specs=[VMEM] * len(outs),
        scratch_shapes=list(scratch.values()),
        compiler_params=params(30),
        cost_estimate=pl.CostEstimate(
            flops=(12 if kind == "all" else 6) * rows * width * width,
            bytes_accessed=8 * 2**20,
            transcendentals=rows * HEADS * 640,
        ),
        name="window_" + kind,
    )(*arrays.values())
    return dict(zip(outs, done))


def crps_kernel(count, gathered, target, grad):
    groups, local, share, lanes = gathered.shape
    members = groups * local
    first = lax.axis_index("ens") * share

    def piece(i, total):
        at = pl.ds(pl.multiple_of(i * 16, 16), 16)
        out = []
        for half in range(2):
            cut = slice(half * 8, half * 8 + 8)
            goal = target[pl.ds(pl.multiple_of(first + i * 16 + half * 8, 8), 8)]
            pred = [gathered[m // local, m % local, at].astype(F32)[cut] for m in range(members)]
            slopes = [None] * members
            spread = jnp.zeros_like(goal)
            pull = []
            for a in range(members):
                delta = pred[a] - goal
                square = delta * delta + SMOOTH * SMOOTH
                inv = lax.rsqrt(square)
                pull.append(delta * inv)
                total = total + square * inv
                for b in range(a + 1, members):
                    delta = pred[a] - pred[b]
                    square = delta * delta + SMOOTH * SMOOTH
                    inv = lax.rsqrt(square)
                    f = delta * inv
                    spread = spread + square * inv
                    slopes[a] = f if slopes[a] is None else slopes[a] + f
                    slopes[b] = -f if slopes[b] is None else slopes[b] - f
            total = total - (2.0 * spread + members * SMOOTH) / (2 * (members - 1))
            out.append([pull[a] - slopes[a] / (members - 1) for a in range(members)])
        for m in range(members):
            to = pl.ds(pl.multiple_of(m % local * share + i * 16, 16), 16)
            grad[m // local, to] = jnp.concatenate([out[0][m], out[1][m]], 0).astype(BF)
        return total

    total = lax.fori_loop(0, share // 16, piece, jnp.zeros((8, lanes), F32))
    terms = split(jnp.sum(total, axis=0, keepdims=True) * (1.0 / count), 3)
    row = lax.broadcasted_iota(jnp.int32, (TAIL, lanes), 0)
    tail = jnp.zeros((TAIL, lanes), F32)
    for i, term in enumerate(terms):
        tail = jnp.where(row == i, term.astype(F32), tail)
    for i in range(groups):
        grad[i, local * share :] = tail.astype(BF)


def crps(gathered, target, count):
    groups, local, share, lanes = gathered.shape
    return pl.pallas_call(
        functools.partial(crps_kernel, count),
        out_shape=jax.ShapeDtypeStruct((groups, local * share + TAIL, lanes), BF),
        in_specs=[VMEM, VMEM],
        out_specs=VMEM,
        compiler_params=params(8),
        name="fair_crps",
    )(gathered, target)


def back_kernel(members, slopes, w_decode, grad):
    shares, held, lanes = slopes.shape
    share = (held - TAIL) // members
    steps = pl.num_programs(0) // members
    each = shares // steps
    step = pl.program_id(0)
    at = pl.ds(pl.multiple_of(step // steps * share, 16), share)
    rows = slopes[pl.ds(step % steps * each, each), at].reshape(each * share, lanes)
    grad[0] = lax.dot_general(rows, w_decode[...], NT, preferred_element_type=F32).astype(BF)


def back(slopes, w_decode, members):
    shares, held, lanes = slopes.shape
    share = (held - TAIL) // members
    width = w_decode.shape[0]
    steps = 2
    rows = shares * share
    return pl.pallas_call(
        functools.partial(back_kernel, members),
        grid=(members * steps,),
        out_shape=jax.ShapeDtypeStruct((members, rows, width), BF),
        in_specs=[
            pl.BlockSpec(slopes.shape, lambda i: (0, 0, 0)),
            pl.BlockSpec(w_decode.shape, lambda i: (0, 0)),
        ],
        out_specs=pl.BlockSpec((1, rows // steps, width), lambda i: (i // steps, i % steps, 0)),
        compiler_params=params(12),
        cost_estimate=pl.CostEstimate(
            flops=2 * members * rows * width * lanes, bytes_accessed=3 * 2**20, transcendentals=0
        ),
        name="state_grad",
    )(slopes, w_decode)


def body(states, member_noise, w_query, w_key, w_value, w_out, w_decode, target):
    members, rows, width = states.shape
    ens, space = lax.axis_size("ens"), lax.axis_size("space")
    cross = [(i, i + 1) for i in range(1, space - 1, 2)]
    chip = [(i, i + 1) for i in range(0, space, 2)]
    both = lambda pairs: pairs + [(j, i) for i, j in pairs]
    far, near, member_noise, w_query = edges(states, member_noise, w_query)
    outer = lax.ppermute(far, "space", both(cross))
    inner = lax.ppermute(near, "space", both(chip))
    query, keys, values, w_key, w_value = qkv(
        states, member_noise, w_query, w_key, w_value
    )
    own = dict(noise=member_noise, query=query, keys=keys, values=values)
    halo = dict(inner=inner, outer=outer, w_key=w_key, w_value=w_value)
    begun = attend("own", 0, ens, states=states, w_out=w_out, w_decode=w_decode, **own)
    done = attend("halo", 0, ens, **own, **halo, **begun)["forecast"]
    for m in range(1, members):
        done = attend(
            "all", m, ens, states=states, w_decode=w_decode, earlier=done,
            w_both=begun["w_both"], **own, **halo,
        )["forecast"]
    gathered = lax.all_to_all(done, "ens", 0, 0)
    count = members * ens * rows * space * w_decode.shape[1]
    slopes = lax.all_to_all(crps(gathered, target, count), "ens", 0, 0)
    held = slopes.shape[1] - TAIL
    part = jnp.sum(slopes[:, held : held + 3].astype(F32), axis=(0, 1))
    parts = lax.all_to_all(jnp.broadcast_to(part, (space, 1, part.shape[0])), "space", 0, 0)
    return back(slopes, w_decode, members), jnp.sum(parts)


def solution(mesh):
    in_specs = (P("ens", "space", None), P("ens", None), P(), P(), P(), P(), P(), P("space", None))
    out_specs = (P("ens", "space", None), P())
    return jax.shard_map(body, mesh=mesh, in_specs=in_specs, out_specs=out_specs, check_vma=False)
```

```python
import functools
import math
import types

import jax
import jax.numpy as jnp
from jax import lax
from jax.experimental import pallas as pl
from jax.experimental.pallas import tpu as pltpu
from jax.sharding import PartitionSpec as P

HEADS = 16
WIN = 256
SMOOTH = 0.25
EPS = 1e-5
SUB = 128
UNROLL = {"own": 8, "halo": 8, "all": 8}
AHEAD = {"own": 1, "halo": 2, "all": 0}
CHUNK = {"own": 4, "halo": 2, "all": 5}
TAIL = 16
LOW, HIGH = 2.0**-80, 2.0**100
BF, F32 = jnp.bfloat16, jnp.float32
VMEM = pl.BlockSpec(memory_space=pltpu.VMEM)
HBM = pl.BlockSpec(memory_space=pltpu.HBM)
NT = (((1,), (1,)), ((), ()))


def params(mib):
    return pltpu.CompilerParams(vmem_limit_bytes=mib * 2**20)


def normed(rows, noise):
    hidden = rows.astype(F32) + noise
    return (hidden * lax.rsqrt(jnp.mean(hidden * hidden, axis=-1, keepdims=True) + EPS)).astype(BF)


def split(x, terms):
    parts = []
    for _ in range(terms):
        parts.append(x.astype(BF))
        x = x - parts[-1].astype(F32)
    return parts


def edges_kernel(states, noise, w_query, far, near, shift, held_query, sems):
    rows = states.shape[1]
    even = lax.axis_index("space") % 2 == 0
    first, last = pl.ds(0, WIN), pl.ds(rows - WIN, WIN)

    def move(out, back):
        copies = [
            pltpu.make_async_copy(states.at[:, out], far, sems.at[0]),
            pltpu.make_async_copy(states.at[:, back], near, sems.at[1]),
            pltpu.make_async_copy(noise, shift, sems.at[2]),
            pltpu.make_async_copy(w_query, held_query, sems.at[3]),
        ]
        for copy in copies:
            copy.start()
        for copy in copies:
            copy.wait()

    @pl.when(even)
    def _():
        move(first, last)

    @pl.when(~even)
    def _():
        move(last, first)


def edges(states, noise, w_query):
    members, _, width = states.shape
    return pl.pallas_call(
        edges_kernel,
        out_shape=[
            jax.ShapeDtypeStruct((members, WIN, width), BF),
            jax.ShapeDtypeStruct((members, WIN, width), BF),
            pltpu.VMEM(noise.shape, F32),
            pltpu.VMEM(w_query.shape, BF),
        ],
        in_specs=[HBM] * 3,
        out_specs=[VMEM] * 4,
        scratch_shapes=[pltpu.SemaphoreType.DMA((4,))],
        compiler_params=params(4),
        name="edges",
    )(*[pltpu.with_memory_space_constraint(x, pltpu.HBM) for x in (states, noise, w_query)])


def qkv_kernel(
    states, noise, w_query, w_key, w_value, query, keys, values, held_key, held_value,
    norm, sems,
):
    members, rows, width = states.shape
    scale = 1.0 / math.sqrt(width // HEADS)
    step = 256
    pieces = [(m, pl.ds(i * step, step)) for m in range(members) for i in range(rows // step)]
    moves = [(w_key, held_key), (w_value, held_value)]
    copies = [pltpu.make_async_copy(a, b, sems.at[i]) for i, (a, b) in enumerate(moves)]
    for copy in copies:
        copy.start()
    for m, at in pieces[:1]:
        norm[m, at] = normed(states[m, at], noise[m : m + 1])
    for i, (m, at) in enumerate(pieces):
        x = norm[m, at]
        query[m, at] = (jnp.dot(x, w_query[...], preferred_element_type=F32) * scale).astype(BF)
        for later, part in pieces[i + 1 : i + 2]:
            norm[later, part] = normed(states[later, part], noise[later : later + 1])
    copies[0].wait()
    for m, at in pieces:
        keys[m, at] = jnp.dot(norm[m, at], held_key[...], preferred_element_type=F32).astype(BF)
    copies[1].wait()
    for m, at in pieces:
        values[m, at] = jnp.dot(norm[m, at], held_value[...], preferred_element_type=F32).astype(BF)


def qkv(states, noise, w_query, w_key, w_value):
    members, rows, width = states.shape
    return pl.pallas_call(
        qkv_kernel,
        out_shape=[jax.ShapeDtypeStruct(states.shape, BF)] * 3
        + [pltpu.VMEM(x.shape, BF) for x in (w_key, w_value)],
        in_specs=[VMEM] * 3 + [HBM] * 2,
        out_specs=[VMEM] * 5,
        scratch_shapes=[
            pltpu.VMEM(states.shape, BF),
            pltpu.SemaphoreType.DMA((2,)),
        ],
        compiler_params=params(20),
        cost_estimate=pl.CostEstimate(
            flops=6 * members * rows * width * width, bytes_accessed=8 * 2**20, transcendentals=0
        ),
        name="own_qkv",
    )(states, noise, w_query, *[pltpu.with_memory_space_constraint(x, pltpu.HBM) for x in (w_key, w_value)])


def attend_kernel(kind, m, names, *refs):
    r = types.SimpleNamespace(**dict(zip(names, refs)))
    query, keys, values = r.query, r.keys, r.values
    kk, vv = r.kk, r.vv
    unroll = UNROLL[kind]
    members, rows, width = query.shape
    pairs = width // SUB
    subs = rows // SUB
    pad = WIN // SUB
    span = 2 * pad + 1
    total = subs + 2 * pad
    inside = [j for j in range(total) if pad <= j < pad + subs]
    held = {"own": inside, "halo": [j for j in range(total) if j not in inside]}
    held = held.get(kind, list(range(total)))
    lane = lax.broadcasted_iota(jnp.int32, (SUB, SUB), 1)
    row = lax.broadcasted_iota(jnp.int32, (SUB, SUB), 0)
    left = lane < SUB // 2
    zero = jnp.zeros((SUB, SUB), BF)
    one = jnp.ones((SUB, SUB), BF)
    place = lax.axis_index("space")
    even = place % 2 == 0
    starts = place == 0
    ends = place == lax.axis_size("space") - 1

    def absent(j):
        return starts if j < pad else ends

    def outside(j):
        return j not in inside

    for u in range(unroll):
        for n, j in enumerate(held):
            unit = jnp.where(absent(j), zero, one) if outside(j) else one
            at = 2 * SUB * n
            vv[u, at : at + SUB, SUB:] = jnp.where(left, unit, zero)
            vv[u, at + SUB : at + 2 * SUB, SUB:] = jnp.where(left, zero, unit)

    def source(m, inner, halo, j, c):
        if j < pad:
            return halo[j * SUB : (j + 1) * SUB, c]
        if j < pad + subs:
            return inner[m, (j - pad) * SUB : (j - pad + 1) * SUB, c]
        return halo[(j - subs) * SUB : (j - subs + 1) * SUB, c]

    halo_k, halo_v = (None, None) if kind == "own" else (r.halo_k, r.halo_v)

    def pack(m, u, pair):
        c = pl.ds(pl.multiple_of(pair * SUB, SUB), SUB)
        for n, j in enumerate(held):
            at = 2 * SUB * n
            key = source(m, keys, halo_k, j, c)
            value = source(m, values, halo_v, j, c)
            if outside(j):
                value = jnp.where(absent(j), zero, value)
            kk[u, at : at + SUB] = jnp.where(left, key, zero)
            kk[u, at + SUB : at + 2 * SUB] = jnp.where(left, zero, key)
            vv[u, at : at + SUB, :SUB] = jnp.where(left, value, zero)
            vv[u, at + SUB : at + 2 * SUB, :SUB] = jnp.where(left, zero, value)

    def masked(s, j):
        if j == 0:
            return jnp.where(lane >= row, s, -1e30)
        if j == span - 1:
            return jnp.where(lane <= row, s, -1e30)
        return s

    def chunks(a):
        window = [j for j in range(a, a + span) if j in held]
        return [window[i : i + CHUNK[kind]] for i in range(0, len(window), CHUNK[kind])]

    def packed(window):
        first = held.index(window[0])
        return slice(2 * SUB * first, 2 * SUB * (first + len(window)))

    def weigh(m, u, pair, a, window):
        c = pl.ds(pl.multiple_of(pair * SUB, SUB), SUB)
        own = slice(a * SUB, (a + 1) * SUB)
        at = packed(window)
        s = lax.dot_general(query[m, own, c], kk[u, at], NT, preferred_element_type=F32)
        parts = []
        for n, j in enumerate(window):
            for k in range(2 * n, 2 * n + 2):
                parts.append(jnp.exp(masked(s[:, k * SUB : (k + 1) * SUB], j - a)).astype(BF))
        return jnp.concatenate(parts, axis=1)

    def mix(u, window, weights):
        return jnp.dot(weights, vv[u, packed(window)], preferred_element_type=F32)

    def store(pair, a, o):
        c = pl.ds(pl.multiple_of(pair * SUB, SUB), SUB)
        own = slice(a * SUB, (a + 1) * SUB)
        if kind == "own":
            r.partial[pair, own] = o
            return
        if kind == "halo":
            o = o + r.partial[pair, own]
        norms = o[:, SUB:]
        r.mixed[own, c] = (o[:, :SUB] / norms).astype(BF)
        r.bad[...] = jnp.where((norms > LOW) & (norms < HIGH), r.bad[...], 1.0)

    def safe_block(m, pair, a):
        c = pl.ds(pl.multiple_of(pair * SUB, SUB), SUB)
        q = query[m, a * SUB : (a + 1) * SUB, c]
        outs = []
        for side in range(2):
            mine = left if side == 0 else ~left
            scores, vals = [], []
            for j in range(a, a + span):
                key = source(m, keys, halo_k, j, c)
                own = jnp.where(mine, q, zero)
                s = lax.dot_general(own, key, NT, preferred_element_type=F32)
                s = masked(s, j - a)
                if outside(j):
                    s = jnp.where(absent(j), -1e30, s)
                scores.append(s)
                vals.append(source(m, values, halo_v, j, c))
            s = jnp.concatenate(scores, axis=1)
            p = jnp.exp(s - jnp.max(s, axis=-1, keepdims=True))
            norms = jnp.sum(p, axis=-1, keepdims=True)
            outs.append(
                jnp.dot(
                    (p / norms).astype(BF),
                    jnp.concatenate(vals, axis=0),
                    preferred_element_type=F32,
                )
            )
        r.mixed[a * SUB : (a + 1) * SUB, c] = jnp.where(left, outs[0], outs[1]).astype(BF)

    def heads(i, _):
        for u in range(unroll):
            pack(m, u, i * unroll + u)
        steps = [(u, a, w) for u in range(unroll) for a in range(subs) for w in chunks(a)]
        ready, sums = [], {}
        for n in range(len(steps) + AHEAD[kind]):
            if n < len(steps):
                u, a, window = steps[n]
                ready.append(weigh(m, u, i * unroll + u, a, window))
            if n >= AHEAD[kind]:
                u, a, window = steps[n - AHEAD[kind]]
                o = mix(u, window, ready[n - AHEAD[kind]])
                o = sums[u, a] + o if (u, a) in sums else o
                sums[u, a] = o
                if window == chunks(a)[-1]:
                    store(i * unroll + u, a, o)
        return 0

    shift = r.noise[m : m + 1]
    if kind == "own":
        lanes = r.w_decode.shape[1]
        for i in range(members):
            terms = [jnp.broadcast_to(x, (8, width)) for x in split(r.noise[i : i + 1], 3)]
            constant = jnp.dot(
                jnp.concatenate(terms, axis=0), r.w_decode[...], preferred_element_type=F32
            )
            constant = constant[0:1] + constant[8:9] + constant[16:17]
            r.base[i] = constant + jnp.dot(
                r.states[i], r.w_decode[...], preferred_element_type=F32
            )
        product = jnp.dot(r.w_out[...], r.w_decode[...], preferred_element_type=F32)
        r.w_both[:, :lanes], r.w_both[:, lanes:] = split(product, 2)
        lax.fori_loop(0, pairs // unroll, heads, 0)
        return

    for side in range(2):
        x = normed(jnp.where(even == (side == 0), r.outer[m], r.inner[m]), shift)
        at = slice(side * WIN, (side + 1) * WIN)
        halo_k[at] = jnp.dot(x, r.w_key[...], preferred_element_type=F32).astype(BF)
        halo_v[at] = jnp.dot(x, r.w_value[...], preferred_element_type=F32).astype(BF)
    r.bad[...] = jnp.zeros_like(r.bad)
    for i in range(m):
        r.forecast[:, i] = r.earlier[:, i]

    def finish():
        forecast = r.forecast
        lanes = forecast.shape[3]
        share = rows // forecast.shape[0]
        for i in range(rows // 256):
            at = slice(i * 256, (i + 1) * 256)
            out = jnp.dot(r.mixed[at], r.w_both[...], preferred_element_type=F32)
            out = out[:, :lanes] + out[:, lanes:] + r.base[m, at]
            each = 256 // share
            forecast[i * each : (i + 1) * each, m] = out.astype(BF).reshape(each, share, -1)

    lax.fori_loop(0, pairs // unroll, heads, 0)
    finish()

    @pl.when(jnp.max(r.bad[...]) > 0.0)
    def _():
        def again(pair, _):
            for a in range(subs):
                safe_block(m, pair, a)
            return 0

        lax.fori_loop(0, pairs, again, 0)
        finish()


def attend(kind, m, shares, **arrays):
    members, rows, width = arrays["query"].shape
    lanes = arrays["w_decode" if kind == "own" else "base"].shape[-1]
    keep = {"own": rows, "halo": 2 * WIN}.get(kind, 2 * WIN + rows)
    base = (members, rows, lanes)
    unroll = UNROLL[kind]
    ready = {"forecast": jax.ShapeDtypeStruct((shares, members, rows // shares, lanes), BF)}
    begun = {
        "partial": jax.ShapeDtypeStruct((width // SUB, rows, 2 * SUB), F32),
        "w_both": jax.ShapeDtypeStruct((width, 2 * lanes), BF),
        "base": jax.ShapeDtypeStruct(base, F32),
    }
    scratch = {
        "kk": pltpu.VMEM((unroll, 2 * keep, SUB), BF),
        "vv": pltpu.VMEM((unroll, 2 * keep, 2 * SUB), BF),
    }
    if kind != "own":
        scratch["halo_k"] = scratch["halo_v"] = pltpu.VMEM((2 * WIN, width), BF)
        scratch["mixed"] = pltpu.VMEM((rows, width), BF)
        scratch["bad"] = pltpu.VMEM((SUB, SUB), F32)
    outs = begun if kind == "own" else ready
    names = [*arrays, *outs, *scratch]
    done = pl.pallas_call(
        functools.partial(attend_kernel, kind, m, names),
        out_shape=list(outs.values()),
        in_specs=[VMEM] * len(arrays),
        out_specs=[VMEM] * len(outs),
        scratch_shapes=list(scratch.values()),
        compiler_params=params(30),
        cost_estimate=pl.CostEstimate(
            flops=(12 if kind == "all" else 6) * rows * width * width,
            bytes_accessed=8 * 2**20,
            transcendentals=rows * HEADS * 640,
        ),
        name="window_" + kind,
    )(*arrays.values())
    return dict(zip(outs, done))


def crps_kernel(count, gathered, target, grad):
    groups, local, share, lanes = gathered.shape
    members = groups * local
    first = lax.axis_index("ens") * share

    def piece(i, total):
        at = pl.ds(pl.multiple_of(i * 16, 16), 16)
        out = []
        for half in range(2):
            cut = slice(half * 8, half * 8 + 8)
            goal = target[pl.ds(pl.multiple_of(first + i * 16 + half * 8, 8), 8)]
            pred = [gathered[m // local, m % local, at].astype(F32)[cut] for m in range(members)]
            slopes = [None] * members
            spread = jnp.zeros_like(goal)
            pull = []
            for a in range(members):
                delta = pred[a] - goal
                square = delta * delta + SMOOTH * SMOOTH
                inv = lax.rsqrt(square)
                pull.append(delta * inv)
                total = total + square * inv
                for b in range(a + 1, members):
                    delta = pred[a] - pred[b]
                    square = delta * delta + SMOOTH * SMOOTH
                    inv = lax.rsqrt(square)
                    f = delta * inv
                    spread = spread + square * inv
                    slopes[a] = f if slopes[a] is None else slopes[a] + f
                    slopes[b] = -f if slopes[b] is None else slopes[b] - f
            total = total - (2.0 * spread + members * SMOOTH) / (2 * (members - 1))
            out.append([pull[a] - slopes[a] / (members - 1) for a in range(members)])
        for m in range(members):
            to = pl.ds(pl.multiple_of(m % local * share + i * 16, 16), 16)
            grad[m // local, to] = jnp.concatenate([out[0][m], out[1][m]], 0).astype(BF)
        return total

    total = lax.fori_loop(0, share // 16, piece, jnp.zeros((8, lanes), F32))
    terms = split(jnp.sum(total, axis=0, keepdims=True) * (1.0 / count), 3)
    row = lax.broadcasted_iota(jnp.int32, (TAIL, lanes), 0)
    tail = jnp.zeros((TAIL, lanes), F32)
    for i, term in enumerate(terms):
        tail = jnp.where(row == i, term.astype(F32), tail)
    for i in range(groups):
        grad[i, local * share :] = tail.astype(BF)


def crps(gathered, target, count):
    groups, local, share, lanes = gathered.shape
    return pl.pallas_call(
        functools.partial(crps_kernel, count),
        out_shape=jax.ShapeDtypeStruct((groups, local * share + TAIL, lanes), BF),
        in_specs=[VMEM, VMEM],
        out_specs=VMEM,
        compiler_params=params(8),
        name="fair_crps",
    )(gathered, target)


def back_kernel(members, slopes, w_decode, grad):
    shares, held, lanes = slopes.shape
    share = (held - TAIL) // members
    steps = pl.num_programs(0) // members
    each = shares // steps
    step = pl.program_id(0)
    at = pl.ds(pl.multiple_of(step // steps * share, 16), share)
    rows = slopes[pl.ds(step % steps * each, each), at].reshape(each * share, lanes)
    grad[0] = lax.dot_general(rows, w_decode[...], NT, preferred_element_type=F32).astype(BF)


def back(slopes, w_decode, members):
    shares, held, lanes = slopes.shape
    share = (held - TAIL) // members
    width = w_decode.shape[0]
    steps = 2
    rows = shares * share
    return pl.pallas_call(
        functools.partial(back_kernel, members),
        grid=(members * steps,),
        out_shape=jax.ShapeDtypeStruct((members, rows, width), BF),
        in_specs=[
            pl.BlockSpec(slopes.shape, lambda i: (0, 0, 0)),
            pl.BlockSpec(w_decode.shape, lambda i: (0, 0)),
        ],
        out_specs=pl.BlockSpec((1, rows // steps, width), lambda i: (i // steps, i % steps, 0)),
        compiler_params=params(12),
        cost_estimate=pl.CostEstimate(
            flops=2 * members * rows * width * lanes, bytes_accessed=3 * 2**20, transcendentals=0
        ),
        name="state_grad",
    )(slopes, w_decode)


def body(states, member_noise, w_query, w_key, w_value, w_out, w_decode, target):
    members, rows, width = states.shape
    ens, space = lax.axis_size("ens"), lax.axis_size("space")
    cross = [(i, i + 1) for i in range(1, space - 1, 2)]
    chip = [(i, i + 1) for i in range(0, space, 2)]
    both = lambda pairs: pairs + [(j, i) for i, j in pairs]
    far, near, member_noise, w_query = edges(states, member_noise, w_query)
    outer = lax.ppermute(far, "space", both(cross))
    inner = lax.ppermute(near, "space", both(chip))
    query, keys, values, w_key, w_value = qkv(
        states, member_noise, w_query, w_key, w_value
    )
    own = dict(noise=member_noise, query=query, keys=keys, values=values)
    halo = dict(inner=inner, outer=outer, w_key=w_key, w_value=w_value)
    begun = attend("own", 0, ens, states=states, w_out=w_out, w_decode=w_decode, **own)
    done = attend("halo", 0, ens, **own, **halo, **begun)["forecast"]
    for m in range(1, members):
        done = attend(
            "all", m, ens, earlier=done, w_both=begun["w_both"], base=begun["base"], **own, **halo
        )["forecast"]
    gathered = lax.all_to_all(done, "ens", 0, 0)
    count = members * ens * rows * space * w_decode.shape[1]
    slopes = lax.all_to_all(crps(gathered, target, count), "ens", 0, 0)
    held = slopes.shape[1] - TAIL
    part = jnp.sum(slopes[:, held : held + 3].astype(F32), axis=(0, 1))
    parts = lax.all_to_all(jnp.broadcast_to(part, (space, 1, part.shape[0])), "space", 0, 0)
    return back(slopes, w_decode, members), jnp.sum(parts)


def solution(mesh):
    in_specs = (P("ens", "space", None), P("ens", None), P(), P(), P(), P(), P(), P("space", None))
    out_specs = (P("ens", "space", None), P())
    return jax.shard_map(body, mesh=mesh, in_specs=in_specs, out_specs=out_specs, check_vma=False)
```
